256 devices in a mesh: prow: 32 (over z, x), pcol: 8 (over y, core).
Axes of the slice: x: 4, y: 4, z: 8, core: 2. Of those that a mesh axis runs over, the one named last changes fastest.
Arguments:
- root_cov: float32 [4096, 4096], P('prow', 'pcol'), as said below
- row_blocks: int32 [4, 16], replicated, may hold values from 8 to 63, as said below
- lhat_t: float32 [4, 1024, 2048], P(None, 'prow', 'pcol'), may hold values from -0.25 to 0.25
- diag_inv: float32 [4, 1024, 1024], P(None, None, 'pcol'), as said below
Outputs:
- row_panels: float32 [4, 1024, 2048], P(None, None, 'pcol')
- diag_blocks: float32 [4, 1024, 1024], P(None, None, 'pcol')
The draws below stay inside these ranges and needn't reach their ends.
Inputs may be any that keep to these rules, and one draw needn't show every extreme that they name: `row_blocks`: each row lists 16 distinct blocks. Row 0 holds blocks of the ancestor region only, two of each residue modulo 8, always including block 63; row k > 0 holds all 8 blocks of supernode k - 1 and one block of each residue modulo 8 from row k - 1. Within a row the blocks are ordered by residue modulo 8, then ascending. `root_cov`: symmetric with a positive diagonal. `diag_inv`: each supernode's block is symmetric with a positive diagonal.
All inputs are finite; a program needn't handle non-finite values.
Results may differ from the reference program's by a relative error of at most 0.00012.
Values sent between devices are 32-bit elements; how exact they have to be, the bound alone decides.
A program may use at most 64 MiB of HBM per device.

```python
import jax
import jax.numpy as jnp
from jax import lax

BLOCK = 128
SUPER_BLOCKS = 8
SUPERS = 4
ROOT_BLOCKS = 32
NB = 64
W = 1024
K = 16
GRID_ROWS = 32
GRID_COLS = 8
N_PROW = 32
N_PCOL = 8


def symmetric_block(key, order, low, high, spread):
    key_off, key_diag = jax.random.split(key, 2)
    off = jax.random.normal(key_off, (order, order), jnp.float32)
    off = (off + off.T) * (spread / order ** 0.5)
    diag = jax.random.uniform(key_diag, (order,), jnp.float32, low, high)
    where_diag = jnp.arange(order)[:, None] == jnp.arange(order)[None, :]
    whole = jnp.where(where_diag, diag[None, :], off)
    return whole


def to_store(natural_ordering, row_block_list, column_blocks, process_grid_rows, process_grid_cols):
    shaped = natural_ordering.reshape(row_block_list // process_grid_rows, process_grid_rows, BLOCK, column_blocks // process_grid_cols, process_grid_cols, BLOCK)
    return shaped.transpose(1, 0, 2, 4, 3, 5).reshape(row_block_list * BLOCK, column_blocks * BLOCK)


def draw_root_cov(key, part):
    key = jax.random.fold_in(key, 5)
    whole = symmetric_block(key, ROOT_BLOCKS * BLOCK, 1.5, 3.0, 0.7)
    return to_store(whole, ROOT_BLOCKS, ROOT_BLOCKS, GRID_ROWS, GRID_COLS)


def draw_diag_inv(key, part):
    key = jax.random.fold_in(key, 7)
    blocks = []
    for k in range(SUPERS):
        whole = symmetric_block(jax.random.fold_in(key, k), W, 2.0, 4.0, 0.7)
        blocks.append(to_store(whole, SUPER_BLOCKS, SUPER_BLOCKS, GRID_COLS, GRID_COLS))
    return jnp.stack(blocks)


def draw_row_blocks(key, part):
    key = jax.random.fold_in(key, 9)
    key_pick, key_flip = jax.random.split(key)
    per_class = ROOT_BLOCKS // SUPER_BLOCKS
    scores = jax.random.randint(key_pick, (SUPER_BLOCKS, per_class), 0, 1 << 20) * per_class + jnp.arange(per_class)[None, :]
    order = jnp.argsort(scores, axis=1)
    first = order[:, 0]
    second = order[:, 1]
    is_last = jnp.arange(SUPER_BLOCKS) == SUPER_BLOCKS - 1
    last_other = jnp.where(first == per_class - 1, second, first)
    first = jnp.where(is_last, per_class - 1, first)
    second = jnp.where(is_last, last_other, second)
    lead = SUPERS * SUPER_BLOCKS
    classes = jnp.arange(SUPER_BLOCKS)
    current = jnp.stack([lead + classes + SUPER_BLOCKS * first, lead + classes + SUPER_BLOCKS * second], axis=1)
    flips = jax.random.randint(key_flip, (SUPERS, SUPER_BLOCKS), 0, 2)
    rows = []
    for k in range(SUPERS):
        if k > 0:
            prev_start = (SUPERS - k) * SUPER_BLOCKS
            keep = jnp.where(flips[k] == 0, current[:, 0], current[:, 1])
            current = jnp.stack([prev_start + classes, keep], axis=1)
        flat = current.reshape(-1)
        keyed = flat % GRID_COLS * (4 * NB) + flat
        rows.append(flat[jnp.argsort(keyed)])
    return jnp.stack(rows).astype(jnp.int32)


def steps_of(rng, extent, shards, low, high):
    gain = 1.0
    for dim, shards_of in shards:
        draws = jax.random.uniform(jax.random.fold_in(jax.random.fold_in(rng, 6), dim), (shards_of,), jnp.float32, low / len(shards), high / len(shards))
        gain = gain * jnp.repeat(jnp.exp(draws), extent[dim] // shards_of).reshape((-1,) + (1,) * (len(extent) - 1 - dim))
    return gain


def normal_values(stream_key, extent, deviation, most, pieces=(), held_as=jnp.bfloat16):
    gain = steps_of(stream_key, extent, pieces, -0.22, 0.18) if pieces else 1.0
    values = jax.random.normal(stream_key, extent, jnp.float32) * deviation * gain
    return jnp.minimum(jnp.maximum(values, -most), most).astype(held_as)


def setup_inputs(seed: int = 0) -> dict:
    keys = jax.random.split(jax.random.key(seed), 5)
    root_cov = draw_root_cov(jax.random.fold_in(keys[4], 71), 0)
    row_blocks = draw_row_blocks(jax.random.fold_in(keys[4], 71), 0)
    lhat_t = normal_values(keys[2], (SUPERS, W, K * BLOCK), (K * 32) ** -0.5, 0.25, ((1, 32), (2, 8)), jnp.float32)
    diag_inv = draw_diag_inv(jax.random.fold_in(keys[4], 71), 0)
    return dict(root_cov=root_cov, row_blocks=row_blocks, lhat_t=lhat_t, diag_inv=diag_inv)


def unblock(store, row_block_list, column_blocks, process_grid_rows, process_grid_cols):
    shaped = store.reshape(process_grid_rows, row_block_list // process_grid_rows, BLOCK, process_grid_cols, column_blocks // process_grid_cols, BLOCK)
    return shaped.transpose(1, 0, 2, 4, 3, 5).reshape(row_block_list * BLOCK, column_blocks * BLOCK)


def regroup_blocks(natural_ordering, row_block_list, column_blocks, process_grid_rows, process_grid_cols):
    shaped = natural_ordering.reshape(row_block_list // process_grid_rows, process_grid_rows, BLOCK, column_blocks // process_grid_cols, process_grid_cols, BLOCK)
    return shaped.transpose(1, 0, 2, 4, 3, 5).reshape(row_block_list * BLOCK, column_blocks * BLOCK)


def rows_natural(store):
    shaped = store.reshape(N_PCOL, SUPER_BLOCKS // N_PCOL, BLOCK, store.shape[1])
    return shaped.transpose(1, 0, 2, 3).reshape(W, store.shape[1])


def rows_storage(natural_ordering):
    shaped = natural_ordering.reshape(SUPER_BLOCKS // N_PCOL, N_PCOL, BLOCK, natural_ordering.shape[1])
    return shaped.transpose(1, 0, 2, 3).reshape(W, natural_ordering.shape[1])


def reference(root_cov, row_blocks, lhat_t, diag_inv):
    high = lax.Precision.HIGHEST
    lead = SUPERS * SUPER_BLOCKS
    root = unblock(root_cov, ROOT_BLOCKS, ROOT_BLOCKS, N_PROW, N_PCOL)
    root_blk = root.reshape(ROOT_BLOCKS, BLOCK, ROOT_BLOCKS, BLOCK).transpose(0, 2, 1, 3)
    upper = jnp.zeros((lead, NB, BLOCK, BLOCK), jnp.float32)
    panels = []
    diagonal_list = []
    for k in range(SUPERS):
        start = (SUPERS - 1 - k) * SUPER_BLOCKS
        index = row_blocks[k].astype(jnp.int32)
        left = index[:, None] + jnp.zeros((1, K), jnp.int32)
        right = index[None, :] + jnp.zeros((K, 1), jnp.int32)
        lower_idx = jnp.minimum(left, right)
        from_row = upper[jnp.clip(left, 0, lead - 1), right]
        from_col = jnp.swapaxes(upper[jnp.clip(right, 0, lead - 1), left], -1, -2)
        from_root = root_blk[jnp.clip(left - lead, 0, ROOT_BLOCKS - 1), jnp.clip(right - lead, 0, ROOT_BLOCKS - 1)]
        stored = jnp.where((left <= right)[:, :, None, None], from_row, from_col)
        blocks = jnp.where((lower_idx < lead)[:, :, None, None], stored, from_root)
        matrix = blocks.transpose(0, 2, 1, 3).reshape(K * BLOCK, K * BLOCK)
        lhat = rows_natural(lhat_t[k])
        panel = -jnp.dot(matrix, lhat.T, precision=high)
        gram = jnp.dot(lhat, panel, precision=high)
        diagonal_unpermuted = unblock(diag_inv[k], SUPER_BLOCKS, SUPER_BLOCKS, N_PCOL, N_PCOL) - gram
        turned = panel.T
        upper = upper.at[start + jnp.arange(SUPER_BLOCKS)[:, None], index[None, :]].set(
            turned.reshape(SUPER_BLOCKS, BLOCK, K, BLOCK).transpose(0, 2, 1, 3))
        upper = upper.at[start:start + SUPER_BLOCKS, start:start + SUPER_BLOCKS].set(
            diagonal_unpermuted.reshape(SUPER_BLOCKS, BLOCK, SUPER_BLOCKS, BLOCK).transpose(0, 2, 1, 3))
        panels.append(rows_storage(turned))
        diagonal_list.append(regroup_blocks(diagonal_unpermuted, SUPER_BLOCKS, SUPER_BLOCKS, N_PCOL, N_PCOL))
    return jnp.stack(panels), jnp.stack(diagonal_list)
```

```python
import functools

import jax
import jax.numpy as jnp
from jax import lax
from jax.experimental import pallas as pl
from jax.experimental.pallas import tpu as pltpu
from jax.sharding import PartitionSpec as P

MESH = pl.DeviceIdType.MESH
NZ = 8
NX = 4
NQ = 8
F32 = jnp.float32
BF16 = jnp.bfloat16


def dev(p, q):
    return {"prow": p, "pcol": q}


def copy_to(src, dst, send, recv, device):
    return pltpu.make_async_remote_copy(
        src_ref=src, dst_ref=dst, send_sem=send, recv_sem=recv, device_id=device, device_id_type=MESH
    )


def halves(x):
    hi = x.astype(BF16)
    lo = (x - hi.astype(F32)).astype(BF16)
    return hi, lo


def dot_nn(a, b):
    return jnp.dot(a, b, preferred_element_type=F32)


def dot_nt(a, b):
    return lax.dot_general(a, b, (((1,), (1,)), ((), ())), preferred_element_type=F32)


def kernel(
    rb, root, lhat, dinv, xo, do,
    cls_out, cls_in, lrow, lsp, quad, turn, gs, gr, dloc,
    z_recv, x_recv, ag_send, cls_sem, row_sem, g_sem, t_sem, d_sem,
):
    p = lax.axis_index("prow")
    q = lax.axis_index("pcol")
    z, x = p // NX, p % NX
    r = p % NQ
    j = z // 2

    dcopy = pltpu.make_async_copy(dinv.at[:, pl.ds(pl.multiple_of(p * 32, 32), 32), :], dloc, d_sem)
    dcopy.start()

    barrier = pltpu.get_barrier_semaphore()

    def hail_z(d, c):
        pl.semaphore_signal(barrier, inc=1, device_id=dev((z + d) % NZ * NX + x, q), device_id_type=MESH)
        return c

    def hail_x(d, c):
        pl.semaphore_signal(barrier, inc=1, device_id=dev(z * NX + (x + d) % NX, q), device_id_type=MESH)
        return c

    def hail_q(d, c):
        pl.semaphore_signal(barrier, inc=1, device_id=dev(p, (q + d) % NQ), device_id_type=MESH)
        return c

    lax.fori_loop(1, NZ, hail_z, 0)
    lax.fori_loop(1, NX, hail_x, 0)
    lax.fori_loop(1, NQ, hail_q, 0)

    slot = [rb[0, 2 * r + t] == 32 + p for t in range(2)]
    for c in range(2):
        mine = rb[0, 2 * q + c]
        col = root[:, 0:128]
        for m in range(1, 4):
            col = jnp.where(mine == 32 + 8 * m + q, root[:, 128 * m : 128 * m + 128], col)
        for t in range(2):
            kept = jnp.where(slot[t], col, jnp.zeros_like(col))
            cls_out[2 * t, c] = kept[0:64]
            cls_out[2 * t + 1, c] = kept[64:128]

    pl.semaphore_wait(barrier, NZ + NX + NQ - 3)

    def class_peer(e, c):
        o = (j + e) % 4
        copy_to(
            cls_out.at[o], cls_in.at[j], cls_sem.at[0], cls_sem.at[1], dev((2 * o + z % 2) * NX + x, q)
        ).start()
        return c

    lax.fori_loop(1, 4, class_peer, 0)

    def row_peer(e, c):
        copy_to(lhat, lrow.at[q], row_sem.at[0], row_sem.at[1], dev(p, (q + e) % NQ)).start()
        return c

    lax.fori_loop(1, NQ, row_peer, 0)
    lrow[q] = lhat[...]

    def chunk_a(zz, xx):
        jj = zz // 2
        rr = zz % 2 * NX + xx
        return quad.at[:, jj // 2, pl.ds(pl.multiple_of(128 * rr + 64 * (jj % 2), 64), 64), :]

    def chunk_x(k, c):
        return lambda zz, xx: xo.at[k, c, pl.ds(pl.multiple_of(32 * (zz * NX + xx), 32), 32), :]

    def chunk_d(k):
        return lambda zz, xx: do.at[k, pl.ds(pl.multiple_of(32 * (zz * NX + xx), 32), 32), :]

    def to_x(chunk, n, zz):
        ref = chunk(zz, x)

        def one(e, c):
            copy_to(ref, ref, ag_send.at[n], x_recv.at[n], dev(z * NX + (x + e) % NX, q)).start()
            return c

        lax.fori_loop(1, NX, one, 0)

    def start_gather(chunk, n):
        ref = chunk(z, x)

        def one(i, c):
            d = (i + 4) % NZ
            d = d + (d == 0) * 4
            copy_to(ref, ref, ag_send.at[n], z_recv.at[n, d], dev((z + d) % NZ * NX + x, q)).start()
            return c

        lax.fori_loop(0, 4, one, 0)
        lax.fori_loop(5, 8, one, 0)
        to_x(chunk, n, z)

    def forward(chunk, n):
        def one(i, c):
            h = i // 2 + 1
            d = h + (i % 2) * (NZ - 2 * h)
            zz = (z + NZ - d) % NZ
            ref = chunk(zz, x)
            copy_to(ref, ref, ag_send.at[n], z_recv.at[n, d], dev(p, q)).wait_recv()
            to_x(chunk, n, zz)
            return c

        lax.fori_loop(0, NZ - 1, one, 0)

    def wait_gather(whole, n):
        copy_to(whole, whole, ag_send.at[n], x_recv.at[n], dev(p, q)).wait_recv()

    def wait_sent(whole, n):
        copy_to(whole, whole, ag_send.at[n], x_recv.at[n], dev(p, q)).wait_send()

    def wait_x(k, c, n):
        wait_gather(xo.at[k, c, pl.ds(0, 768), :], n)

    N_A = 12

    def n_x(k, c):
        return 3 * k + c

    def n_d(k):
        return 3 * k + 2

    part = cls_in.at[pl.ds(0, 3)]
    copy_to(part, part, cls_sem.at[0], cls_sem.at[1], dev(p, q)).wait_recv()
    own = cls_out[j]
    for e in range(1, 4):
        own = own + cls_in[(j + e) % 4]
    quad[:, j // 2, pl.ds(pl.multiple_of(128 * r + 64 * (j % 2), 64), 64), :] = own
    start_gather(chunk_a, N_A)

    part7 = lrow.at[pl.ds(0, 7)]
    copy_to(part7, part7, row_sem.at[0], row_sem.at[1], dev(p, q)).wait_recv()

    def split_rows(k, c):
        for o in range(NQ):
            v = lrow[o, k]
            hi, lo = halves(v)
            for h in range(2):
                lsp[k, h, 0:32, 128 * o : 128 * o + 128] = hi[:, 128 * h : 128 * h + 128]
                lsp[k, h, 32:64, 128 * o : 128 * o + 128] = lo[:, 128 * h : 128 * h + 128]
        return c

    lax.fori_loop(0, 4, split_rows, 0)
    dcopy.wait()
    forward(chunk_a, N_A)
    wait_gather(quad.at[:, :, pl.ds(0, 768), :], N_A)

    def new_x(k, c):
        both = jnp.zeros((64, 128), F32)
        small = jnp.zeros((32, 128), F32)
        for h in range(2):
            hi, lo = halves(quad[c, h])
            both = both + dot_nn(lsp[k, h], hi)
            small = small + dot_nn(lsp[k, h, 0:32], lo)
        xo[k, c, pl.ds(pl.multiple_of(32 * p, 32), 32), :] = -(both[0:32] + both[32:64] + small)
        start_gather(chunk_x(k, c), n_x(k, c))

    new_x(0, 1)
    new_x(0, 0)
    forward(chunk_x(0, 1), n_x(0, 1))
    forward(chunk_x(0, 0), n_x(0, 0))
    wait_sent(quad.at[:, :, pl.ds(0, 992), :], N_A)

    def step(k, carry):
        wait_x(k, 1, n_x(k, 1))
        wait_x(k, 0, n_x(k, 0))
        lh, ll = halves(lhat[k])
        lboth = jnp.concatenate([lh, ll], axis=0)
        for o in range(NQ):
            rows = slice(128 * o, 128 * o + 128)
            xv = jnp.concatenate([xo[k, 0, rows, :], xo[k, 1, rows, :]], axis=1)
            xh, xl = halves(xv)
            g2 = dot_nt(lboth, xh)
            gs[k, o] = g2[0:32] + g2[32:64] + dot_nt(lh, xl)

        def g_peer(e, c):
            o = (q + e) % NQ
            copy_to(gs.at[k, o], gr.at[k, q], g_sem.at[k, 0], g_sem.at[k, 1], dev(p, o)).start()
            return c

        lax.fori_loop(1, NQ, g_peer, 0)
        gr[k, q] = gs[k, q]

        @pl.when(k < 3)
        def _():
            second = rb[k + 1, 2 * q + 1] == rb[k, 2 * q + 1]
            for o in range(NQ):
                rows = slice(128 * o, 128 * o + 128)
                low = rb[k + 1, 2 * o + 1] == rb[k, 2 * o + 1]
                top = jnp.where(second, quad[1, 0, rows, :], quad[0, 0, rows, :])
                bot = jnp.where(second, quad[1, 1, rows, :], quad[0, 1, rows, :])
                quad[1, 1, rows, :] = jnp.where(low, bot, top)
                quad[1, 0, rows, :] = jnp.where(second, xo[k, 1, rows, :], xo[k, 0, rows, :])

            def t_peer(e, c):
                o = (q + e) % NQ
                copy_to(
                    quad.at[1, 0, pl.ds(pl.multiple_of(128 * o, 128), 128), :], turn.at[k, q],
                    t_sem.at[k, 0], t_sem.at[k, 1], dev(p, o),
                ).start()
                return c

            lax.fori_loop(1, NQ, t_peer, 0)
            turn[k, q] = quad[1, 0, pl.ds(pl.multiple_of(128 * q, 128), 128), :]
            new_x(k + 1, 1)

        got = gr.at[k, pl.ds(0, 7)]
        copy_to(got, got, g_sem.at[k, 0], g_sem.at[k, 1], dev(p, q)).wait_recv()
        total = gr[k, 0]
        for o in range(1, NQ):
            total = total + gr[k, o]
        do[k, pl.ds(pl.multiple_of(32 * p, 32), 32), :] = dloc[k] - total
        start_gather(chunk_d(k), n_d(k))

        @pl.when(k < 3)
        def _():
            forward(chunk_x(k + 1, 1), n_x(k + 1, 1))
            got_t = turn.at[k, pl.ds(0, 7)]
            copy_to(got_t, got_t, t_sem.at[k, 0], t_sem.at[k, 1], dev(p, q)).wait()
            for o in range(NQ):
                quad[0, 1, 128 * o : 128 * o + 128, :] = turn[k, o].T

        forward(chunk_d(k), n_d(k))
        wait_gather(do.at[k, pl.ds(0, 768), :], n_d(k))

        @pl.when(k < 3)
        def _():
            quad[0, 0] = do[k]
            new_x(k + 1, 0)
            forward(chunk_x(k + 1, 0), n_x(k + 1, 0))

        return carry

    lax.fori_loop(0, 4, step, 0)

    def finish(k, c):
        wait_sent(xo.at[k, 0, pl.ds(0, 992), :], n_x(k, 0))
        wait_sent(xo.at[k, 1, pl.ds(0, 992), :], n_x(k, 1))
        wait_sent(do.at[k, pl.ds(0, 992), :], n_d(k))
        sent = gr.at[k, pl.ds(0, 7)]
        copy_to(sent, sent, g_sem.at[k, 0], g_sem.at[k, 1], dev(p, q)).wait_send()
        return c

    lax.fori_loop(0, 4, finish, 0)
    copy_to(part, part, cls_sem.at[0], cls_sem.at[1], dev(p, q)).wait_send()
    copy_to(part7, part7, row_sem.at[0], row_sem.at[1], dev(p, q)).wait_send()


def on_device(root_cov, row_blocks, lhat_t, diag_inv):
    vmem = pl.BlockSpec(memory_space=pltpu.VMEM)
    dma = pltpu.SemaphoreType.DMA
    xs, ds = pl.pallas_call(
        kernel,
        out_shape=(
            jax.ShapeDtypeStruct((4, 2, 1024, 128), F32),
            jax.ShapeDtypeStruct((4, 1024, 128), F32),
        ),
        in_specs=[
            pl.BlockSpec(memory_space=pltpu.SMEM),
            vmem,
            vmem,
            pl.BlockSpec(memory_space=pl.ANY),
        ],
        out_specs=(vmem, vmem),
        scratch_shapes=[
            pltpu.VMEM((4, 2, 64, 128), F32),
            pltpu.VMEM((4, 2, 64, 128), F32),
            pltpu.VMEM((8, 4, 32, 256), F32),
            pltpu.VMEM((4, 2, 64, 1024), BF16),
            pltpu.VMEM((2, 2, 1024, 128), F32),
            pltpu.VMEM((3, 8, 128, 128), F32),
            pltpu.VMEM((4, 8, 32, 128), F32),
            pltpu.VMEM((4, 8, 32, 128), F32),
            pltpu.VMEM((4, 32, 128), F32),
            dma((13, 8)),
            dma((13,)),
            dma((13,)),
            dma((2,)),
            dma((2,)),
            dma((4, 2)),
            dma((3, 2)),
            dma,
        ],
        compiler_params=pltpu.CompilerParams(
            collective_id=0, has_side_effects=True, vmem_limit_bytes=48 << 20
        ),
        name="selinv",
    )(row_blocks, root_cov, lhat_t, diag_inv)
    panels = xs.transpose(0, 2, 1, 3).reshape(4, 1024, 256)
    return panels, ds


def solution(mesh):
    return jax.shard_map(
        on_device,
        mesh=mesh,
        in_specs=(P("prow", "pcol"), P(), P(None, "prow", "pcol"), P(None, None, "pcol")),
        out_specs=(P(None, None, "pcol"), P(None, None, "pcol")),
        check_vma=False,
    )
```

```python
import jax
import jax.numpy as jnp
from jax import lax
from jax.experimental import pallas as pl
from jax.experimental.pallas import tpu as pltpu
from jax.sharding import PartitionSpec as P

MESH = pl.DeviceIdType.MESH
NZ = 8
NX = 4
NQ = 8
F32 = jnp.float32
BF16 = jnp.bfloat16


def dev(p, q):
    return {"prow": p, "pcol": q}


def copy_to(src, dst, send, recv, device):
    return pltpu.make_async_remote_copy(
        src_ref=src, dst_ref=dst, send_sem=send, recv_sem=recv, device_id=device, device_id_type=MESH
    )


def halves(x):
    hi = x.astype(BF16)
    lo = (x - hi.astype(F32)).astype(BF16)
    return hi, lo


def stacked(x):
    return jnp.concatenate(halves(x), axis=0)


def dot_nn(a, b):
    return jnp.dot(a, b, preferred_element_type=F32)


def dot_nt(a, b):
    return lax.dot_general(a, b, (((1,), (1,)), ((), ())), preferred_element_type=F32)


def rows(i, n):
    return pl.ds(pl.multiple_of(i * n, n), n)


def kernel(
    rb, root_h, lhat_h, dinv_h, out_x, out_d,
    root, lhat, dblk, dturn, cls_out, cls_in, lrow0, lrow, lx, az, xp, xr, bsel, xsel,
    lc, lsp, ltt, xo, ed, do, turn, gs, gr,
    in_sem, cls_sem, row0_sem, row_sem, lx_sem, az_sem, xr_sem, b_sem, lc_sem, g_sem, t_sem,
    z_recv, x_recv, c_recv, ag_send, o_sem,
):
    p = lax.axis_index("prow")
    q = lax.axis_index("pcol")
    z, x = p // NX, p % NX
    me = dev(p, q)
    par, quarter = z % 2, z // 2

    loads = [
        pltpu.make_async_copy(root_h, root, in_sem.at[0]),
        pltpu.make_async_copy(lhat_h, lhat, in_sem.at[1]),
        pltpu.make_async_copy(dinv_h.at[:, rows(z, 128), :], dblk, in_sem.at[2]),
    ]
    for load in loads:
        load.start()

    def to_z(d):
        return dev((z + d) % NZ * NX + x, q)

    def to_x(e):
        return dev(z * NX + (x + e) % NX, q)

    def to_q(e):
        return dev(p, (q + e) % NQ)

    def loop(a, b, body):
        def run(i, c):
            body(i)
            return c

        lax.fori_loop(a, b, run, 0)

    barrier = pltpu.get_barrier_semaphore()
    loop(1, NZ, lambda d: pl.semaphore_signal(barrier, inc=1, device_id=to_z(d), device_id_type=MESH))
    loop(1, NX, lambda e: pl.semaphore_signal(barrier, inc=1, device_id=to_x(e), device_id_type=MESH))
    loop(1, NQ, lambda e: pl.semaphore_signal(barrier, inc=1, device_id=to_q(e), device_id_type=MESH))

    def got(ref, recv):
        copy_to(ref, ref, recv, recv, me).wait_recv()

    def sent(ref, send):
        copy_to(ref, ref, send, send, me).wait_send()

    loads[0].wait()
    home = par * NX + x
    slot = [rb[0, 2 * home + t] == 32 + p for t in range(2)]
    for c in range(2):
        mine = rb[0, 2 * q + c]
        col = root[:, 0:128]
        for m in range(1, 4):
            col = jnp.where(mine == 32 + 8 * m + q, root[:, 128 * m : 128 * m + 128], col)
        for t in range(2):
            kept = jnp.where(slot[t], col, jnp.zeros_like(col))
            cls_out[2 * t, c] = kept[0:64]
            cls_out[2 * t + 1, c] = kept[64:128]
    loads[1].wait()
    pl.semaphore_wait(barrier, NZ + NX + NQ - 3)

    def class_peer(e):
        o = (quarter + e) % 4
        copy_to(
            cls_out.at[o], cls_in.at[quarter], cls_sem.at[0], cls_sem.at[1], dev((2 * o + par) * NX + x, q)
        ).start()

    loop(1, 4, class_peer)
    qh, qx = q // NX, q % NX
    loop(1, NQ, lambda e: copy_to(lhat.at[0], lrow0.at[qh, qx], row0_sem.at[0], row0_sem.at[1], to_q(e)).start())
    loop(
        1, NQ,
        lambda e: copy_to(lhat.at[pl.ds(1, 3)], lrow.at[q], row_sem.at[0], row_sem.at[1], to_q(e)).start(),
    )
    lrow0[qh, qx] = lhat[0]
    lrow[q] = lhat[1:4]
    for k in range(4):
        lc[k, z] = lhat[k]

    def send_lc(k):
        loop(1, NZ, lambda d: copy_to(lhat.at[k], lc.at[k, z], lc_sem.at[k, 0], lc_sem.at[k, 1], to_z(d)).start())

    def order(i):
        h = i // 2 + 1
        return h + (i % 2) * (NZ - 2 * h)

    got(cls_in.at[pl.ds(0, 3)], cls_sem.at[1])
    own = cls_out[quarter]
    for e in range(1, 4):
        own = own + cls_in[(quarter + e) % 4]
    az_own = az.at[:, par, rows(quarter, 64), :]
    az_own[...] = own
    loop(0, NZ - 1, lambda i: copy_to(az_own, az_own, az_sem.at[0], az_sem.at[1], to_z(order(6 - i))).start())
    send_lc(0)

    got(lrow0.at[0, pl.ds(0, 7)], row0_sem.at[1])

    def lx_peer(e):
        copy_to(lrow0.at[:, (x + e) % NX], lx.at[x], lx_sem.at[0], lx_sem.at[1], to_x(e)).start()

    loop(1, NX, lx_peer)
    lx[x] = lrow0[:, x]

    loads[2].wait()

    def turn_dinv(k):
        dturn[k] = dblk[k].T

    loop(0, 4, turn_dinv)
    got(lrow.at[pl.ds(0, 7)], row_sem.at[1])

    def prepare(k):
        for o in range(NQ):
            for h in range(2):
                v = lrow[o, k, :, 128 * h : 128 * h + 128]
                hi, lo = halves(v)
                lsp[k, h, 0:32, 128 * o : 128 * o + 128] = hi
                lsp[k, h, 32:64, 128 * o : 128 * o + 128] = lo
                ltt[k, h, 128 * o : 128 * o + 128, :] = jnp.concatenate(halves(v.T), axis=1)

    loop(0, 3, prepare)

    def chunk_x(k, c):
        return lambda zz, xx: xo.at[k, c, rows(zz * NX + xx, 32), :]

    def chunk_d(k):
        return lambda zz, xx: ed.at[k, rows(zz * NX + xx, 32), :]

    def n_x(k, c):
        return 3 * k + c

    def n_d(k):
        return 3 * k + 2

    def start_gather(chunk, n):
        ref = chunk(z, x)
        loop(1, NX, lambda e: copy_to(ref, ref, ag_send.at[n], c_recv.at[n], to_x(e)).start())

        def one(i):
            d = order(6 - i)
            copy_to(ref, ref, ag_send.at[n], z_recv.at[n, d], to_z(d)).start()

        loop(0, NZ - 1, one)

    def forward(chunk, n):
        def one(i):
            d = order(i)
            ref = chunk((z + NZ - d) % NZ, x)
            got(ref, z_recv.at[n, d])
            loop(1, NX, lambda e: copy_to(ref, ref, ag_send.at[n], x_recv.at[n], to_x(e)).start())

        loop(0, NZ - 1, one)

    def put_x(k, c, value):
        xo[k, c, rows(p, 32), :] = value
        start_gather(chunk_x(k, c), n_x(k, c))

    got(lx.at[pl.ds(0, 3)], lx_sem.at[1])
    got(az.at[:, :, pl.ds(0, 224), :], az_sem.at[1])
    lefts = [halves(jnp.concatenate([lx[e, h] for e in range(NX)], axis=0)) for h in range(2)]
    for c in range(2):
        total = jnp.zeros((128, 128), F32)
        for h in range(2):
            hi, lo = halves(az[c, h])
            total = total + dot_nn(lefts[h][0], hi) + dot_nn(lefts[h][1], hi) + dot_nn(lefts[h][0], lo)
        for e in range(NX):
            xp[e, c] = total[32 * e : 32 * e + 32]

    def xp_peer(e):
        copy_to(xp.at[(x + e) % NX], xr.at[x], xr_sem.at[0], xr_sem.at[1], to_x(e)).start()

    loop(1, NX, xp_peer)
    xr[x] = xp[x]

    second = rb[1, 2 * q + 1] == rb[0, 2 * q + 1]
    for h in range(2):
        o = x + NX * h
        low = rb[1, 2 * o + 1] == rb[0, 2 * o + 1]
        top = jnp.where(second, az[1, h, 0:128], az[0, h, 0:128])
        bot = jnp.where(second, az[1, h, 128:256], az[0, h, 128:256])
        bsel[h, x] = jnp.where(low, bot, top)
    b_own = bsel.at[:, x]
    loop(1, NX, lambda e: copy_to(b_own, b_own, b_sem.at[0], b_sem.at[1], to_x(e)).start())

    got(xr.at[pl.ds(0, 3)], xr_sem.at[1])
    first = -(xr[0] + xr[1] + xr[2] + xr[3])
    put_x(0, 0, first[0])
    put_x(0, 1, first[1])

    def step(k, carry):
        got(xo.at[k, 1, pl.ds(0, 96), :], c_recv.at[n_x(k, 1)])
        got(lc.at[k, pl.ds(0, 7)], lc_sem.at[k, 1])
        got(xo.at[k, 0, pl.ds(0, 96), :], c_recv.at[n_x(k, 0)])
        xh, xl = halves(jnp.concatenate([xo[k, 0, rows(z, 128), :], xo[k, 1, rows(z, 128), :]], axis=1))
        ch, cl = halves(lc[k].reshape(256, 256))
        part = dot_nt(ch, xh) + dot_nt(cl, xh) + dot_nt(ch, xl)
        gs[k] = part.reshape(NQ, 32, 128)

        def g_peer(e):
            copy_to(gs.at[k, (q + e) % NQ], gr.at[k, q], g_sem.at[k, 0], g_sem.at[k, 1], to_q(e)).start()

        loop(1, NQ, g_peer)
        gr[k, q] = gs[k, q]
        forward(chunk_x(k, 1), n_x(k, 1))
        forward(chunk_x(k, 0), n_x(k, 0))

        got(gr.at[k, pl.ds(0, 7)], g_sem.at[k, 1])
        total = gr[k, 0]
        for o in range(1, NQ):
            total = total + gr[k, o]
        ed[k, rows(p, 32), :] = dturn[k, rows(x, 32), :] - total
        start_gather(chunk_d(k), n_d(k))

        got(xo.at[k, 1, pl.ds(0, 672), :], x_recv.at[n_x(k, 1)])
        got(xo.at[k, 0, pl.ds(0, 672), :], x_recv.at[n_x(k, 0)])

        @pl.when(k < 3)
        def _():
            pick = rb[k + 1, 2 * q + 1] == rb[k, 2 * q + 1]

            @pl.when(k > 0)
            def _():
                for o in range(NQ):
                    lower = rb[k + 1, 2 * o + 1] == rb[k, 2 * o + 1]
                    span = slice(128 * o, 128 * o + 128)
                    upper_part = jnp.where(pick, xsel[span, :], do[k - 1, span, :])
                    lower_part = jnp.where(pick, bsel[o // NX, o % NX], turn[k - 1, o].T)
                    bsel[o // NX, o % NX] = jnp.where(lower, lower_part, upper_part)

            xsel[...] = jnp.where(pick, xo[k, 1], xo[k, 0])

            def t_peer(e):
                copy_to(
                    xsel.at[rows((q + e) % NQ, 128), :], turn.at[k, q], t_sem.at[k, 0], t_sem.at[k, 1], to_q(e)
                ).start()

            loop(1, NQ, t_peer)
            turn[k, q] = xsel[rows(q, 128), :]

        forward(chunk_d(k), n_d(k))
        for c in range(2):
            pltpu.make_async_copy(
                xo.at[k, c], out_x.at[k, :, pl.ds(128 * c, 128)], o_sem.at[k, c]
            ).start()

        @pl.when(k < 3)
        def _():
            send_lc(k + 1)

            @pl.when(k == 0)
            def _():
                got(bsel.at[:, pl.ds(0, 3)], b_sem.at[1])
                sent(bsel.at[:, pl.ds(0, 3)], b_sem.at[0])

            both = jnp.zeros((64, 128), F32)
            small = jnp.zeros((32, 128), F32)
            for h in range(2):
                hi, lo = halves(xsel[...] if h == 0 else bsel[...].reshape(1024, 128))
                both = both + dot_nn(lsp[k, h], hi)
                small = small + dot_nn(lsp[k, h, 0:32], lo)
            put_x(k + 1, 1, -(both[0:32] + both[32:64] + small))
            got(turn.at[k, pl.ds(0, 7)], t_sem.at[k, 1])
            sent(turn.at[k, pl.ds(0, 7)], t_sem.at[k, 0])

        got(ed.at[k, pl.ds(0, 96), :], c_recv.at[n_d(k)])
        got(ed.at[k, pl.ds(0, 672), :], x_recv.at[n_d(k)])

        @pl.when(k < 3)
        def _():
            acc = jnp.zeros((256, 64), F32)
            for o in range(0, NQ, 2):
                wide = slice(128 * o, 128 * o + 256)
                t = jnp.concatenate([turn[k, o], turn[k, o + 1]], axis=1)
                e = jnp.concatenate(
                    [ed[k, 128 * o : 128 * o + 128, :], ed[k, 128 * o + 128 : 128 * o + 256, :]], axis=1
                )
                acc = acc + dot_nn(stacked(t), ltt[k, 1, wide, :]) + dot_nn(stacked(e), ltt[k, 0, wide, :])
            new = acc[0:128, 0:32] + acc[0:128, 32:64] + acc[128:256, 0:32]
            put_x(k + 1, 0, -new.T)

        for o in range(NQ):
            do[k, 128 * o : 128 * o + 128, :] = ed[k, 128 * o : 128 * o + 128, :].T
        pltpu.make_async_copy(do.at[k], out_d.at[k], o_sem.at[k, 2]).start()
        return carry

    lax.fori_loop(0, 4, step, 0)

    def finish(k):
        for c in range(2):
            sent(xo.at[k, c, pl.ds(0, 992), :], ag_send.at[n_x(k, c)])
            pltpu.make_async_copy(xo.at[k, c], out_x.at[k, :, pl.ds(128 * c, 128)], o_sem.at[k, c]).wait()
        sent(ed.at[k, pl.ds(0, 992), :], ag_send.at[n_d(k)])
        sent(gr.at[k, pl.ds(0, 7)], g_sem.at[k, 0])
        sent(lc.at[k, pl.ds(0, 7)], lc_sem.at[k, 0])
        pltpu.make_async_copy(do.at[k], out_d.at[k], o_sem.at[k, 2]).wait()

    loop(0, 4, finish)
    sent(cls_in.at[pl.ds(0, 3)], cls_sem.at[0])
    sent(lrow0.at[0, pl.ds(0, 7)], row0_sem.at[0])
    sent(lrow.at[pl.ds(0, 7)], row_sem.at[0])
    sent(lx.at[pl.ds(0, 3)], lx_sem.at[0])
    sent(az.at[:, :, pl.ds(0, 224), :], az_sem.at[0])
    sent(xr.at[pl.ds(0, 3)], xr_sem.at[0])


def on_device(root_cov, row_blocks, lhat_t, diag_inv):
    anywhere = pl.BlockSpec(memory_space=pl.ANY)
    dma = pltpu.SemaphoreType.DMA
    vmem = pltpu.VMEM
    return pl.pallas_call(
        kernel,
        out_shape=(
            jax.ShapeDtypeStruct((4, 1024, 256), F32),
            jax.ShapeDtypeStruct((4, 1024, 128), F32),
        ),
        in_specs=[pl.BlockSpec(memory_space=pltpu.SMEM), anywhere, anywhere, anywhere],
        out_specs=(anywhere, anywhere),
        scratch_shapes=[
            vmem((128, 512), F32),
            vmem((4, 32, 256), F32),
            vmem((4, 128, 128), F32),
            vmem((4, 128, 128), F32),
            vmem((4, 2, 64, 128), F32),
            vmem((4, 2, 64, 128), F32),
            vmem((2, 8, 32, 256), F32),
            vmem((8, 3, 32, 256), F32),
            vmem((4, 2, 32, 256), F32),
            vmem((2, 2, 256, 128), F32),
            vmem((4, 2, 32, 128), F32),
            vmem((4, 2, 32, 128), F32),
            vmem((2, 4, 128, 128), F32),
            vmem((1024, 128), F32),
            vmem((4, 8, 32, 256), F32),
            vmem((3, 2, 64, 1024), BF16),
            vmem((3, 2, 1024, 64), BF16),
            vmem((4, 2, 1024, 128), F32),
            vmem((4, 1024, 128), F32),
            vmem((4, 1024, 128), F32),
            vmem((3, 8, 128, 128), F32),
            vmem((4, 8, 32, 128), F32),
            vmem((4, 8, 32, 128), F32),
            dma((3,)),
            dma((2,)),
            dma((2,)),
            dma((2,)),
            dma((2,)),
            dma((2,)),
            dma((2,)),
            dma((2,)),
            dma((4, 2)),
            dma((4, 2)),
            dma((3, 2)),
            dma((12, 8)),
            dma((12,)),
            dma((12,)),
            dma((12,)),
            dma((4, 3)),
        ],
        compiler_params=pltpu.CompilerParams(
            collective_id=0, has_side_effects=True, vmem_limit_bytes=60 << 20
        ),
        name="selinv",
    )(row_blocks, root_cov, lhat_t, diag_inv)


def solution(mesh):
    return jax.shard_map(
        on_device,
        mesh=mesh,
        in_specs=(P("prow", "pcol"), P(), P(None, "prow", "pcol"), P(None, None, "pcol")),
        out_specs=(P(None, None, "pcol"), P(None, None, "pcol")),
        check_vma=False,
    )
```

```python
import jax
import jax.numpy as jnp
from jax import lax
from jax.experimental import pallas as pl
from jax.experimental.pallas import tpu as pltpu
from jax.sharding import PartitionSpec as P

MESH = pl.DeviceIdType.MESH
NZ = 8
NX = 4
NQ = 8
F32 = jnp.float32
BF16 = jnp.bfloat16
KEEP = (32, 32, 32)
EARLY = 4


def dev(p, q):
    return {"prow": p, "pcol": q}


def copy_to(src, dst, send, recv, device):
    return pltpu.make_async_remote_copy(
        src_ref=src, dst_ref=dst, send_sem=send, recv_sem=recv, device_id=device, device_id_type=MESH
    )


def halves(x):
    hi = x.astype(BF16)
    lo = (x - hi.astype(F32)).astype(BF16)
    return hi, lo


def stacked(x):
    return jnp.concatenate(halves(x), axis=0)


def dot_nn(a, b):
    return jnp.dot(a, b, preferred_element_type=F32)


def dot_nt(a, b):
    return lax.dot_general(a, b, (((1,), (1,)), ((), ())), preferred_element_type=F32)


def rows(i, n):
    return pl.ds(pl.multiple_of(i * n, n), n)


def kernel(
    rb, root_h, lhat_h, dinv_h, out_x, out_d,
    root, lhat, dblk, dturn, cls, lrow0, lrow, lx, az, xp, xr, bsel, xsel,
    lc, lsp, ltt, xo, ed, do, turn, gs, gr, held, tall,
    in_sem, cls_sem, row0_sem, row_sem, lx_sem, xr_sem, b_sem, lc_send, lc_recv, g_sem, t_sem,
    z_recv, x_recv, c_recv, b_recv, ag_send, o_sem,
):
    p = lax.axis_index("prow")
    q = lax.axis_index("pcol")
    z, x = p // NX, p % NX
    me = dev(p, q)
    par, quarter = z % 2, z // 2

    loads = [
        pltpu.make_async_copy(root_h, root, in_sem.at[0]),
        pltpu.make_async_copy(lhat_h, lhat, in_sem.at[1]),
        pltpu.make_async_copy(dinv_h.at[:, rows(z, 128), :], dblk, in_sem.at[2]),
    ]
    for load in loads:
        load.start()

    def to_z(d):
        return dev((z + d) % NZ * NX + x, q)

    def to_x(e):
        return dev(z * NX + (x + e) % NX, q)

    def to_q(e):
        return dev(p, (q + e) % NQ)

    def loop(a, b, body):
        def run(i, c):
            body(i)
            return c

        lax.fori_loop(a, b, run, 0)

    barrier = pltpu.get_barrier_semaphore()
    loop(1, NZ, lambda d: pl.semaphore_signal(barrier, inc=1, device_id=to_z(d), device_id_type=MESH))
    loop(1, NX, lambda e: pl.semaphore_signal(barrier, inc=1, device_id=to_x(e), device_id_type=MESH))
    loop(1, NQ, lambda e: pl.semaphore_signal(barrier, inc=1, device_id=to_q(e), device_id_type=MESH))

    loop(
        1, NX,
        lambda e: pl.semaphore_signal(
            barrier, inc=1, device_id=dev((2 * quarter + 1 - par) * NX + (x + e) % NX, q), device_id_type=MESH
        ),
    )

    def got(ref, recv):
        copy_to(ref, ref, recv, recv, me).wait_recv()

    def sent(ref, send):
        copy_to(ref, ref, send, send, me).wait_send()

    loads[0].wait()
    g = par * NX + x
    for c in range(2):
        mine = rb[0, 2 * q + c]
        col = root[:, 0:128]
        for m in range(1, 4):
            col = jnp.where(mine == 32 + 8 * m + q, root[:, 128 * m : 128 * m + 128], col)
        cls[quarter, c] = col
    loads[1].wait()
    pl.semaphore_wait(barrier, NZ + NX + NQ)

    def class_peer(e):
        ref = cls.at[quarter]
        copy_to(ref, ref, cls_sem.at[0], cls_sem.at[1], to_z(2 * e)).start()

    class_peer(2)
    class_peer(1)
    class_peer(3)
    loop(1, NQ, lambda e: copy_to(lhat.at[0], lrow0.at[q], row0_sem.at[0], row0_sem.at[1], to_q(e)).start())
    loop(
        1, NQ,
        lambda e: copy_to(lhat.at[pl.ds(1, 3)], lrow.at[q], row_sem.at[0], row_sem.at[1], to_q(e)).start(),
    )
    lrow0[q] = lhat[0]
    lrow[q] = lhat[1:4]
    for k in range(4):
        lc[k, z] = lhat[k]

    def lc_hop(k, far):
        for side, d in ((0, 1), (1, NZ - 1)):
            if far == 3 and side == 1:
                continue
            ref = lc.at[k, (z + NZ - far * d) % NZ]
            if far > 0:
                got(ref, lc_recv.at[k, side, far - 1])
            copy_to(ref, ref, lc_send.at[k], lc_recv.at[k, side, far], to_z(d)).start()

    def got_lc(k):
        got(lc.at[k, 0], lc_recv.at[k, 1, 2])
        got(lc.at[k, 0], lc_recv.at[k, 0, 3])

    def order(i):
        h = i // 2 + 1
        return h + (i % 2) * (NZ - 2 * h)

    got(lrow0.at[pl.ds(0, 7)], row0_sem.at[1])

    def to_group(e, body):
        o = (g + e) % NQ
        body(o, dev((2 * quarter + o // NX) * NX + o % NX, q))

    def lx_peer(e):
        to_group(
            e, lambda o, d: copy_to(lrow0.at[o], lx.at[g], lx_sem.at[0], lx_sem.at[1], d).start()
        )

    loop(1, NQ, lx_peer)
    lx[g] = lrow0[g]
    lc_hop(0, 0)

    def turn_dinv(k):
        dturn[k] = dblk[k].T


    def prepare(k):
        for o in range(NQ):
            for h in range(2):
                hi, lo = halves(lrow[o, k, :, 128 * h : 128 * h + 128])
                lsp[k, h, 0:32, 128 * o : 128 * o + 128] = hi
                lsp[k, h, 32:64, 128 * o : 128 * o + 128] = lo

    def prepare_t(k):
        for o in range(NQ):
            for h in range(2):
                v = lrow[o, k, :, 128 * h : 128 * h + 128]
                ltt[k, h, 128 * o : 128 * o + 128, :] = jnp.concatenate(halves(v.T), axis=1)

    def buf_of(k, c):
        return (xo.at[k, c], 3 * k + c, KEEP[c]) if c < 2 else (ed.at[k], 3 * k + 2, KEEP[2])

    def start_gather(k, c):
        buf, n, keep = buf_of(k, c)
        ref = buf.at[z, x]
        loop(1, NX, lambda e: copy_to(ref, ref, ag_send.at[n], c_recv.at[n], to_x(e)).start())
        top = buf.at[z, x, pl.ds(0, keep), :]

        def one(i):
            d = order(6 - i)
            copy_to(top, top, ag_send.at[n], z_recv.at[n, d], to_z(d)).start()

        loop(0, NZ - 1, one)

    def got_near(k, c):
        buf, n, keep = buf_of(k, c)
        got(buf.at[0, pl.ds(0, 3)], c_recv.at[n])

    def second_part(k, c):
        buf, n, keep = buf_of(k, c)
        if keep < 32:
            ref = buf.at[z, :, pl.ds(keep, 32 - keep), :]
            loop(
                0, NZ - 1,
                lambda i: copy_to(ref, ref, ag_send.at[n], b_recv.at[n], to_z(order(6 - i))).start(),
            )

    def forward(k, c, first, last):
        buf, n, keep = buf_of(k, c)

        def one(i):
            d = order(i)
            ref = buf.at[(z + NZ - d) % NZ, x, pl.ds(0, keep), :]
            got(ref, z_recv.at[n, d])
            loop(1, NX, lambda e: copy_to(ref, ref, ag_send.at[n], x_recv.at[n], to_x(e)).start())

        loop(first, last, one)

    def got_all(k, c):
        buf, n, keep = buf_of(k, c)
        got(buf.at[pl.ds(0, 7), pl.ds(0, 3), pl.ds(0, keep), :], x_recv.at[n])
        if keep < 32:
            got(buf.at[pl.ds(0, 7), :, pl.ds(keep, 32 - keep), :], b_recv.at[n])

    def put_x(k, c, value):
        xo[k, c, z, x] = value
        start_gather(k, c)

    got(lx.at[pl.ds(0, 7)], lx_sem.at[1])
    left, left_low = halves(lx[...].reshape(256, 256))
    got(cls.at[pl.ds(0, 3)], cls_sem.at[1])
    lc_hop(0, 1)
    for c in range(2):
        for t in range(2):
            want = rb[0, 2 * g + t]
            blk = cls[0, c]
            for o in range(1, 4):
                blk = jnp.where(want == 32 + 8 * o + g, cls[o, c], blk)
            az[c, 128 * t : 128 * t + 128, :] = blk
        hi, lo = halves(az[c])
        total = dot_nn(left, hi) + dot_nn(left_low, hi) + dot_nn(left, lo)
        xp[:, c] = total.reshape(NQ, 32, 128)

    def xp_peer(e):
        to_group(e, lambda o, d: copy_to(xp.at[o], xr.at[g], xr_sem.at[0], xr_sem.at[1], d).start())

    loop(1, NQ, xp_peer)
    xr[g] = xp[g]

    second = rb[1, 2 * q + 1] == rb[0, 2 * q + 1]
    low = rb[1, 2 * g + 1] == rb[0, 2 * g + 1]
    top = jnp.where(second, az[1, 0:128], az[0, 0:128])
    bot = jnp.where(second, az[1, 128:256], az[0, 128:256])
    bsel[g] = jnp.where(low, bot, top)
    b_own = bsel.at[g]

    def b_peer(e):
        to_group(e, lambda o, d: copy_to(b_own, b_own, b_sem.at[0], b_sem.at[1], d).start())

    loads[2].wait()
    loop(0, 4, turn_dinv)
    got(lrow.at[pl.ds(0, 7)], row_sem.at[1])
    prepare(0)
    prepare_t(0)
    lc_hop(0, 2)
    got(xr.at[pl.ds(0, 7)], xr_sem.at[1])
    first = -xr[0]
    for o in range(1, NQ):
        first = first - xr[o]
    lc_hop(0, 3)
    put_x(0, 0, first[0])
    put_x(0, 1, first[1])
    loop(1, NQ, b_peer)

    def times_split(left_rows, value):
        hi, lo = halves(value)
        both = dot_nn(left_rows[...], hi)
        return both[0:32] + both[32:64] + dot_nn(left_rows[0:32], lo)

    def times_turned(right, lefts):
        acc = jnp.zeros((256, 64), F32)
        for i, v in enumerate(lefts):
            acc = acc + dot_nn(stacked(v), right[256 * i : 256 * i + 256, :])
        return acc[0:128, 0:32] + acc[0:128, 32:64] + acc[128:256, 0:32]

    def step(k, carry):
        if KEEP[1] == 32:
            got_near(k, 1)
        else:

            @pl.when(k == 0)
            def _():
                got_near(k, 1)

        got_near(k, 0)
        got_lc(k)
        xh, xl = halves(
            jnp.concatenate([xo[k, 0, z].reshape(128, 128), xo[k, 1, z].reshape(128, 128)], axis=1)
        )
        ch, cl = halves(lc[k].reshape(256, 256))
        part = dot_nt(ch, xh) + dot_nt(cl, xh) + dot_nt(ch, xl)
        gs[k] = part.reshape(NQ, 32, 128)

        def g_peer(e):
            copy_to(gs.at[k, (q + e) % NQ], gr.at[k, q], g_sem.at[k, 0], g_sem.at[k, 1], to_q(e)).start()

        loop(1, NQ, g_peer)
        gr[k, q] = gs[k, q]
        second_part(k, 0)

        @pl.when(k == 0)
        def _():
            second_part(k, 1)
            forward(k, 1, 0, 7)

        forward(k, 0, 0, 7)

        @pl.when(k < 3)
        def _():
            lc_hop(k + 1, 0)

        @pl.when(k == 0)
        def _():
            got(bsel.at[pl.ds(0, 7)], b_sem.at[1])
            sent(bsel.at[pl.ds(0, 7)], b_sem.at[0])
            held[...] = times_split(lsp.at[0, 1], bsel[...].reshape(1024, 128))

        got(gr.at[k, pl.ds(0, 7)], g_sem.at[k, 1])
        total = gr[k, 0]
        for o in range(1, NQ):
            total = total + gr[k, o]
        ed[k, z, x] = dturn[k, rows(x, 32), :] - total
        start_gather(k, 2)
        forward(k, 2, 0, EARLY)
        if KEEP[2] < 32:
            got_near(k, 2)
            second_part(k, 2)

        @pl.when(k < 3)
        def _():
            lc_hop(k + 1, 1)

        got_all(k, 1)
        got_all(k, 0)

        @pl.when(k < 3)
        def _():
            pick = rb[k + 1, 2 * q + 1] == rb[k, 2 * q + 1]
            xsel[...] = jnp.where(pick, xo[k, 1].reshape(1024, 128), xo[k, 0].reshape(1024, 128))

            def t_peer(e):
                copy_to(
                    xsel.at[rows((q + e) % NQ, 128), :], turn.at[k, q], t_sem.at[k, 0], t_sem.at[k, 1], to_q(e)
                ).start()

            loop(1, NQ, t_peer)
            turn[k, q] = xsel[rows(q, 128), :]
            put_x(k + 1, 1, -(held[...] + times_split(lsp.at[k, 0], xsel[...])))

        forward(k, 2, EARLY, 7)
        for c in range(2):
            pltpu.make_async_copy(
                xo.at[k, c], out_x.at[k, :, :, :, pl.ds(128 * c, 128)], o_sem.at[k, c]
            ).start()

        @pl.when(k < 2)
        def _():
            prepare(k + 1)
            prepare_t(k + 1)

        @pl.when(k < 3)
        def _():
            lc_hop(k + 1, 2)
            got(turn.at[k, pl.ds(0, 7)], t_sem.at[k, 1])
            sent(turn.at[k, pl.ds(0, 7)], t_sem.at[k, 0])
            tall[...] = times_turned(
                ltt.at[k, 1], [jnp.concatenate([turn[k, o], turn[k, o + 1]], axis=1) for o in range(0, NQ, 2)]
            )
            lc_hop(k + 1, 3)
            if KEEP[1] < 32:
                got_near(k + 1, 1)
                second_part(k + 1, 1)

        if KEEP[2] == 32:
            got_near(k, 2)
        got_all(k, 2)

        @pl.when(k < 3)
        def _():
            new = tall[...] + times_turned(
                ltt.at[k, 0],
                [
                    jnp.concatenate([ed[k, o].reshape(128, 128), ed[k, o + 1].reshape(128, 128)], axis=1)
                    for o in range(0, NQ, 2)
                ],
            )
            put_x(k + 1, 0, -new.T)
            forward(k + 1, 1, 0, 7)

        for o in range(NQ):
            do[k, 128 * o : 128 * o + 128, :] = ed[k, o].reshape(128, 128).T
        pltpu.make_async_copy(do.at[k], out_d.at[k], o_sem.at[k, 2]).start()

        @pl.when(k < 2)
        def _():
            pick = rb[k + 2, 2 * q + 1] == rb[k + 1, 2 * q + 1]
            for o in range(NQ):
                lower = rb[k + 2, 2 * o + 1] == rb[k + 1, 2 * o + 1]
                span = slice(128 * o, 128 * o + 128)
                upper_part = jnp.where(pick, xsel[span, :], do[k, span, :])
                lower_part = jnp.where(pick, bsel[o], turn[k, o].T)
                bsel[o] = jnp.where(lower, lower_part, upper_part)
            held[...] = times_split(lsp.at[k + 1, 1], bsel[...].reshape(1024, 128))

        return carry

    lax.fori_loop(0, 4, step, 0)

    def finish(k):
        for c in range(3):
            sent(do.at[k, pl.ds(0, 992), :], ag_send.at[3 * k + c])
        for c in range(2):
            pltpu.make_async_copy(
                xo.at[k, c], out_x.at[k, :, :, :, pl.ds(128 * c, 128)], o_sem.at[k, c]
            ).wait()
        sent(gr.at[k, pl.ds(0, 7)], g_sem.at[k, 0])
        sent(lc.at[k, pl.ds(0, 7)], lc_send.at[k])
        pltpu.make_async_copy(do.at[k], out_d.at[k], o_sem.at[k, 2]).wait()

    loop(0, 4, finish)
    sent(cls.at[pl.ds(0, 3)], cls_sem.at[0])
    sent(lrow0.at[pl.ds(0, 7)], row0_sem.at[0])
    sent(lrow.at[pl.ds(0, 7)], row_sem.at[0])
    sent(lx.at[pl.ds(0, 7)], lx_sem.at[0])
    sent(xr.at[pl.ds(0, 7)], xr_sem.at[0])


def hand_over(xs, ds, out_x, out_d, buf_x, buf_d, in_sem, out_sem):
    reads, writes = [], []
    for k in range(4):
        for i in range(2):
            part = pl.ds(4 * i, 4)
            reads.append(pltpu.make_async_copy(xs.at[k, part], buf_x.at[k, part], in_sem.at[k, i]))
            writes.append(pltpu.make_async_copy(buf_x.at[k, part], out_x.at[k, part], out_sem.at[k, i]))
        reads.append(pltpu.make_async_copy(ds.at[k], buf_d.at[k], in_sem.at[k, 2]))
        writes.append(pltpu.make_async_copy(buf_d.at[k], out_d.at[k], out_sem.at[k, 2]))
    for read in reads:
        read.start()
    for read, write in zip(reads, writes):
        read.wait()
        write.start()
    for write in writes:
        write.wait()


def on_device(root_cov, row_blocks, lhat_t, diag_inv):
    anywhere = pl.BlockSpec(memory_space=pl.ANY)
    dma = pltpu.SemaphoreType.DMA
    vmem = pltpu.VMEM
    panels, diagonal = pl.pallas_call(
        kernel,
        out_shape=(
            jax.ShapeDtypeStruct((4, NZ, NX, 32, 256), F32),
            jax.ShapeDtypeStruct((4, 1024, 128), F32),
        ),
        in_specs=[pl.BlockSpec(memory_space=pltpu.SMEM), anywhere, anywhere, anywhere],
        out_specs=(anywhere, anywhere),
        scratch_shapes=[
            vmem((128, 512), F32),
            vmem((4, 32, 256), F32),
            vmem((4, 128, 128), F32),
            vmem((4, 128, 128), F32),
            vmem((4, 2, 128, 128), F32),
            vmem((8, 32, 256), F32),
            vmem((8, 3, 32, 256), F32),
            vmem((8, 32, 256), F32),
            vmem((2, 256, 128), F32),
            vmem((8, 2, 32, 128), F32),
            vmem((8, 2, 32, 128), F32),
            vmem((8, 128, 128), F32),
            vmem((1024, 128), F32),
            vmem((4, 8, 32, 256), F32),
            vmem((3, 2, 64, 1024), BF16),
            vmem((3, 2, 1024, 64), BF16),
            vmem((4, 2, 8, 4, 32, 128), F32),
            vmem((4, 8, 4, 32, 128), F32),
            vmem((4, 1024, 128), F32),
            vmem((3, 8, 128, 128), F32),
            vmem((4, 8, 32, 128), F32),
            vmem((4, 8, 32, 128), F32),
            vmem((32, 128), F32),
            vmem((128, 32), F32),
            dma((3,)),
            dma((2,)),
            dma((2,)),
            dma((2,)),
            dma((2,)),
            dma((2,)),
            dma((2,)),
            dma((4,)),
            dma((4, 2, 4)),
            dma((4, 2)),
            dma((3, 2)),
            dma((12, 8)),
            dma((12,)),
            dma((12,)),
            dma((12,)),
            dma((12,)),
            dma((4, 3)),
        ],
        compiler_params=pltpu.CompilerParams(
            collective_id=0, has_side_effects=True, vmem_limit_bytes=60 << 20
        ),
        name="selinv",
    )(row_blocks, root_cov, lhat_t, diag_inv)
    panels, diagonal = pl.pallas_call(
        hand_over,
        out_shape=(
            jax.ShapeDtypeStruct((4, NZ, NX, 32, 256), F32),
            jax.ShapeDtypeStruct((4, 1024, 128), F32),
        ),
        in_specs=[anywhere, anywhere],
        out_specs=(anywhere, anywhere),
        scratch_shapes=[
            vmem((4, NZ, NX, 32, 256), F32),
            vmem((4, 1024, 128), F32),
            dma((4, 3)),
            dma((4, 3)),
        ],
        compiler_params=pltpu.CompilerParams(vmem_limit_bytes=60 << 20),
        name="hand_over",
    )(panels, diagonal)
    return panels.reshape(4, 1024, 256), diagonal


def solution(mesh):
    return jax.shard_map(
        on_device,
        mesh=mesh,
        in_specs=(P("prow", "pcol"), P(), P(None, "prow", "pcol"), P(None, None, "pcol")),
        out_specs=(P(None, None, "pcol"), P(None, None, "pcol")),
        check_vma=False,
    )
```

```python
import jax
import jax.numpy as jnp
from jax import lax
from jax.experimental import pallas as pl
from jax.experimental.pallas import tpu as pltpu
from jax.sharding import PartitionSpec as P

MESH = pl.DeviceIdType.MESH
NZ = 8
NX = 4
NQ = 8
F32 = jnp.float32
BF16 = jnp.bfloat16
KEEP = (32, 32, 32)
EARLY = 4


def dev(p, q):
    return {"prow": p, "pcol": q}


def copy_to(src, dst, send, recv, device):
    return pltpu.make_async_remote_copy(
        src_ref=src, dst_ref=dst, send_sem=send, recv_sem=recv, device_id=device, device_id_type=MESH
    )


def halves(x):
    hi = x.astype(BF16)
    lo = (x - hi.astype(F32)).astype(BF16)
    return hi, lo


def stacked(x):
    return jnp.concatenate(halves(x), axis=0)


def dot_nn(a, b):
    return jnp.dot(a, b, preferred_element_type=F32)


def dot_nt(a, b):
    return lax.dot_general(a, b, (((1,), (1,)), ((), ())), preferred_element_type=F32)


def rows(i, n):
    return pl.ds(pl.multiple_of(i * n, n), n)


def kernel(
    rb, root_h, lhat_h, dinv_h, out_x, out_d,
    root, lhat, dblk, dturn, cls, lrow0, lrow, lx, az, xp, xr, bsel, xsel,
    lc, lsp, ltt, xo, ed, do, turn, gs, gr, held, tall,
    in_sem, cls_sem, row0_sem, row_sem, lx_sem, xr_sem, b_sem, lc_send, lc_recv, g_sem, t_sem,
    z_recv, x_recv, c_recv, b_recv, ag_send, o_sem,
):
    p = lax.axis_index("prow")
    q = lax.axis_index("pcol")
    z, x = p // NX, p % NX
    me = dev(p, q)
    par, quarter = z % 2, z // 2

    loads = [
        pltpu.make_async_copy(root_h, root, in_sem.at[0]),
        pltpu.make_async_copy(lhat_h, lhat, in_sem.at[1]),
        pltpu.make_async_copy(dinv_h.at[:, rows(z, 128), :], dblk, in_sem.at[2]),
    ]
    for load in loads:
        load.start()

    def to_z(d):
        return dev((z + d) % NZ * NX + x, q)

    def to_x(e):
        return dev(z * NX + (x + e) % NX, q)

    def to_q(e):
        return dev(p, (q + e) % NQ)

    def loop(a, b, body):
        def run(i, c):
            body(i)
            return c

        lax.fori_loop(a, b, run, 0)

    barrier = pltpu.get_barrier_semaphore()
    loop(1, NZ, lambda d: pl.semaphore_signal(barrier, inc=1, device_id=to_z(d), device_id_type=MESH))
    loop(1, NX, lambda e: pl.semaphore_signal(barrier, inc=1, device_id=to_x(e), device_id_type=MESH))
    loop(1, NQ, lambda e: pl.semaphore_signal(barrier, inc=1, device_id=to_q(e), device_id_type=MESH))

    loop(
        1, NX,
        lambda e: pl.semaphore_signal(
            barrier, inc=1, device_id=dev((2 * quarter + 1 - par) * NX + (x + e) % NX, q), device_id_type=MESH
        ),
    )

    def got(ref, recv):
        copy_to(ref, ref, recv, recv, me).wait_recv()

    def sent(ref, send):
        copy_to(ref, ref, send, send, me).wait_send()

    loads[0].wait()
    g = par * NX + x
    for c in range(2):
        mine = rb[0, 2 * q + c]
        col = root[:, 0:128]
        for m in range(1, 4):
            col = jnp.where(mine == 32 + 8 * m + q, root[:, 128 * m : 128 * m + 128], col)
        cls[quarter, c] = col
    loads[1].wait()
    pl.semaphore_wait(barrier, NZ + NX + NQ)

    for c in (1, 0):
        ref = cls.at[quarter, c]
        for e in (2, 1, 3):
            copy_to(ref, ref, cls_sem.at[c, 0], cls_sem.at[c, 1], to_z(2 * e)).start()
    loop(1, NQ, lambda e: copy_to(lhat.at[0], lrow0.at[q], row0_sem.at[0], row0_sem.at[1], to_q(e)).start())
    loop(
        1, NQ,
        lambda e: copy_to(lhat.at[pl.ds(1, 3)], lrow.at[q], row_sem.at[0], row_sem.at[1], to_q(e)).start(),
    )
    lrow0[q] = lhat[0]
    lrow[q] = lhat[1:4]
    for k in range(4):
        lc[k, z] = lhat[k]

    def lc_hop(k, far):
        for side, d in ((0, 1), (1, NZ - 1)):
            if far == 3 and side == 1:
                continue
            ref = lc.at[k, (z + NZ - far * d) % NZ]
            if far > 0:
                got(ref, lc_recv.at[k, side, far - 1])
            copy_to(ref, ref, lc_send.at[k], lc_recv.at[k, side, far], to_z(d)).start()

    def got_lc(k):
        got(lc.at[k, 0], lc_recv.at[k, 1, 2])
        got(lc.at[k, 0], lc_recv.at[k, 0, 3])

    def order(i):
        h = i // 2 + 1
        return h + (i % 2) * (NZ - 2 * h)

    got(lrow0.at[pl.ds(0, 7)], row0_sem.at[1])

    def to_group(e, body):
        o = (g + e) % NQ
        body(o, dev((2 * quarter + o // NX) * NX + o % NX, q))

    def lx_peer(e):
        to_group(
            e, lambda o, d: copy_to(lrow0.at[o], lx.at[g], lx_sem.at[0], lx_sem.at[1], d).start()
        )

    loop(1, NQ, lx_peer)
    lx[g] = lrow0[g]
    lc_hop(0, 0)

    def turn_dinv(k):
        dturn[k] = dblk[k].T


    def prepare(k):
        for o in range(NQ):
            for h in range(2):
                hi, lo = halves(lrow[o, k, :, 128 * h : 128 * h + 128])
                lsp[k, h, 0:32, 128 * o : 128 * o + 128] = hi
                lsp[k, h, 32:64, 128 * o : 128 * o + 128] = lo

    def prepare_t(k):
        for o in range(NQ):
            for h in range(2):
                v = lrow[o, k, :, 128 * h : 128 * h + 128]
                ltt[k, h, 128 * o : 128 * o + 128, :] = jnp.concatenate(halves(v.T), axis=1)

    def buf_of(k, c):
        return (xo.at[k, c], 3 * k + c, KEEP[c]) if c < 2 else (ed.at[k], 3 * k + 2, KEEP[2])

    def start_gather(k, c):
        buf, n, keep = buf_of(k, c)
        ref = buf.at[z, x]
        for e in (2, 1, 3):
            copy_to(ref, ref, ag_send.at[n], c_recv.at[n], to_x(e)).start()
        top = buf.at[z, x, pl.ds(0, keep), :]

        def one(i):
            d = order(6 - i)
            copy_to(top, top, ag_send.at[n], z_recv.at[n, d], to_z(d)).start()

        loop(0, NZ - 1, one)

    def got_near(k, c):
        buf, n, keep = buf_of(k, c)
        got(buf.at[0, pl.ds(0, 3)], c_recv.at[n])

    def second_part(k, c):
        buf, n, keep = buf_of(k, c)
        if keep < 32:
            ref = buf.at[z, :, pl.ds(keep, 32 - keep), :]
            loop(
                0, NZ - 1,
                lambda i: copy_to(ref, ref, ag_send.at[n], b_recv.at[n], to_z(order(6 - i))).start(),
            )

    def forward(k, c, first, last):
        buf, n, keep = buf_of(k, c)

        def one(i):
            d = order(i)
            ref = buf.at[(z + NZ - d) % NZ, x, pl.ds(0, keep), :]
            got(ref, z_recv.at[n, d])
            loop(1, NX, lambda e: copy_to(ref, ref, ag_send.at[n], x_recv.at[n], to_x(e)).start())

        loop(first, last, one)

    def got_all(k, c):
        buf, n, keep = buf_of(k, c)
        got(buf.at[pl.ds(0, 7), pl.ds(0, 3), pl.ds(0, keep), :], x_recv.at[n])
        if keep < 32:
            got(buf.at[pl.ds(0, 7), :, pl.ds(keep, 32 - keep), :], b_recv.at[n])

    def put_x(k, c, value):
        xo[k, c, z, x] = value
        start_gather(k, c)

    got(lx.at[pl.ds(0, 7)], lx_sem.at[1])
    left, left_low = halves(lx[...].reshape(256, 256))
    for c in (1, 0):
        got(cls.at[pl.ds(0, 3), c], cls_sem.at[c, 1])
        if c == 0:
            lc_hop(0, 1)
        for t in range(2):
            want = rb[0, 2 * g + t]
            blk = cls[0, c]
            for o in range(1, 4):
                blk = jnp.where(want == 32 + 8 * o + g, cls[o, c], blk)
            az[c, 128 * t : 128 * t + 128, :] = blk
        hi, lo = halves(az[c])
        total = dot_nn(left, hi) + dot_nn(left_low, hi) + dot_nn(left, lo)
        xp[c] = total.reshape(NQ, 32, 128)
        for e in range(1, NQ):
            to_group(
                e, lambda o, d: copy_to(xp.at[c, o], xr.at[c, g], xr_sem.at[c, 0], xr_sem.at[c, 1], d).start()
            )
        xr[c, g] = xp[c, g]

    second = rb[1, 2 * q + 1] == rb[0, 2 * q + 1]
    low = rb[1, 2 * g + 1] == rb[0, 2 * g + 1]
    top = jnp.where(second, az[1, 0:128], az[0, 0:128])
    bot = jnp.where(second, az[1, 128:256], az[0, 128:256])
    bsel[g] = jnp.where(low, bot, top)
    b_own = bsel.at[g]

    def b_peer(e):
        to_group(e, lambda o, d: copy_to(b_own, b_own, b_sem.at[0], b_sem.at[1], d).start())

    def put_first(c):
        got(xr.at[c, pl.ds(0, 7)], xr_sem.at[c, 1])
        first = -xr[c, 0]
        for o in range(1, NQ):
            first = first - xr[c, o]
        put_x(0, c, first)

    put_first(1)
    loads[2].wait()
    loop(0, 4, turn_dinv)
    got(lrow.at[pl.ds(0, 7)], row_sem.at[1])
    prepare(0)
    prepare_t(0)
    lc_hop(0, 2)
    lc_hop(0, 3)
    put_first(0)
    loop(1, NQ, b_peer)

    def times_split(left_rows, value):
        hi, lo = halves(value)
        both = dot_nn(left_rows[...], hi)
        return both[0:32] + both[32:64] + dot_nn(left_rows[0:32], lo)

    def times_turned(right, lefts):
        acc = jnp.zeros((256, 64), F32)
        for i, v in enumerate(lefts):
            acc = acc + dot_nn(stacked(v), right[256 * i : 256 * i + 256, :])
        return acc[0:128, 0:32] + acc[0:128, 32:64] + acc[128:256, 0:32]

    forward(0, 1, 0, 7)

    def step(k, carry):
        if KEEP[1] == 32:
            got_near(k, 1)
        else:

            @pl.when(k == 0)
            def _():
                got_near(k, 1)

        got_near(k, 0)
        got_lc(k)
        xh, xl = halves(
            jnp.concatenate([xo[k, 0, z].reshape(128, 128), xo[k, 1, z].reshape(128, 128)], axis=1)
        )
        ch, cl = halves(lc[k].reshape(256, 256))
        part = dot_nt(ch, xh) + dot_nt(cl, xh) + dot_nt(ch, xl)
        gs[k] = part.reshape(NQ, 32, 128)

        def g_peer(e):
            copy_to(gs.at[k, (q + e) % NQ], gr.at[k, q], g_sem.at[k, 0], g_sem.at[k, 1], to_q(e)).start()

        for e in (4, 3, 5, 2, 6, 1, 7):
            g_peer(e)
        gr[k, q] = gs[k, q]
        second_part(k, 0)

        @pl.when(k == 0)
        def _():
            second_part(k, 1)

        forward(k, 0, 0, 7)

        @pl.when(k < 3)
        def _():
            lc_hop(k + 1, 0)

        @pl.when(k == 0)
        def _():
            got(bsel.at[pl.ds(0, 7)], b_sem.at[1])
            sent(bsel.at[pl.ds(0, 7)], b_sem.at[0])
            held[...] = times_split(lsp.at[0, 1], bsel[...].reshape(1024, 128))

        got(gr.at[k, pl.ds(0, 7)], g_sem.at[k, 1])
        total = gr[k, 0]
        for o in range(1, NQ):
            total = total + gr[k, o]
        ed[k, z, x] = dturn[k, rows(x, 32), :] - total
        start_gather(k, 2)
        forward(k, 2, 0, EARLY)
        if KEEP[2] < 32:
            got_near(k, 2)
            second_part(k, 2)

        @pl.when(k < 3)
        def _():
            lc_hop(k + 1, 1)

        got_all(k, 1)
        got_all(k, 0)

        @pl.when(k < 3)
        def _():
            pick = rb[k + 1, 2 * q + 1] == rb[k, 2 * q + 1]
            xsel[...] = jnp.where(pick, xo[k, 1].reshape(1024, 128), xo[k, 0].reshape(1024, 128))

            def t_peer(e):
                copy_to(
                    xsel.at[rows((q + e) % NQ, 128), :], turn.at[k, q], t_sem.at[k, 0], t_sem.at[k, 1], to_q(e)
                ).start()

            loop(1, NQ, t_peer)
            turn[k, q] = xsel[rows(q, 128), :]
            put_x(k + 1, 1, -(held[...] + times_split(lsp.at[k, 0], xsel[...])))

        forward(k, 2, EARLY, 7)
        for c in range(2):
            pltpu.make_async_copy(
                xo.at[k, c], out_x.at[k, :, :, :, pl.ds(128 * c, 128)], o_sem.at[k, c]
            ).start()

        @pl.when(k < 2)
        def _():
            prepare(k + 1)
            prepare_t(k + 1)

        @pl.when(k < 3)
        def _():
            lc_hop(k + 1, 2)
            got(turn.at[k, pl.ds(0, 7)], t_sem.at[k, 1])
            sent(turn.at[k, pl.ds(0, 7)], t_sem.at[k, 0])
            tall[...] = times_turned(
                ltt.at[k, 1], [jnp.concatenate([turn[k, o], turn[k, o + 1]], axis=1) for o in range(0, NQ, 2)]
            )
            lc_hop(k + 1, 3)
            if KEEP[1] < 32:
                got_near(k + 1, 1)
                second_part(k + 1, 1)

        if KEEP[2] == 32:
            got_near(k, 2)
        got_all(k, 2)

        @pl.when(k < 3)
        def _():
            new = tall[...] + times_turned(
                ltt.at[k, 0],
                [
                    jnp.concatenate([ed[k, o].reshape(128, 128), ed[k, o + 1].reshape(128, 128)], axis=1)
                    for o in range(0, NQ, 2)
                ],
            )
            put_x(k + 1, 0, -new.T)
            forward(k + 1, 1, 0, 7)

        for o in range(NQ):
            do[k, 128 * o : 128 * o + 128, :] = ed[k, o].reshape(128, 128).T
        pltpu.make_async_copy(do.at[k], out_d.at[k], o_sem.at[k, 2]).start()

        @pl.when(k < 2)
        def _():
            pick = rb[k + 2, 2 * q + 1] == rb[k + 1, 2 * q + 1]
            for o in range(NQ):
                lower = rb[k + 2, 2 * o + 1] == rb[k + 1, 2 * o + 1]
                span = slice(128 * o, 128 * o + 128)
                upper_part = jnp.where(pick, xsel[span, :], do[k, span, :])
                lower_part = jnp.where(pick, bsel[o], turn[k, o].T)
                bsel[o] = jnp.where(lower, lower_part, upper_part)
            held[...] = times_split(lsp.at[k + 1, 1], bsel[...].reshape(1024, 128))

        return carry

    lax.fori_loop(0, 4, step, 0)

    def finish(k):
        for c in range(3):
            sent(do.at[k, pl.ds(0, 992), :], ag_send.at[3 * k + c])
        for c in range(2):
            pltpu.make_async_copy(
                xo.at[k, c], out_x.at[k, :, :, :, pl.ds(128 * c, 128)], o_sem.at[k, c]
            ).wait()
        sent(gr.at[k, pl.ds(0, 7)], g_sem.at[k, 0])
        sent(lc.at[k, pl.ds(0, 7)], lc_send.at[k])
        pltpu.make_async_copy(do.at[k], out_d.at[k], o_sem.at[k, 2]).wait()

    loop(0, 4, finish)
    for c in range(2):
        sent(cls.at[pl.ds(0, 3), c], cls_sem.at[c, 0])
        sent(xr.at[c, pl.ds(0, 7)], xr_sem.at[c, 0])
    sent(lrow0.at[pl.ds(0, 7)], row0_sem.at[0])
    sent(lrow.at[pl.ds(0, 7)], row_sem.at[0])
    sent(lx.at[pl.ds(0, 7)], lx_sem.at[0])


def hand_over(xs, ds, out_x, out_d, buf_x, buf_d, in_sem, out_sem):
    reads, writes = [], []

    def move(src, buf, dst):
        n = len(reads)
        reads.append(pltpu.make_async_copy(src, buf, in_sem.at[n]))
        writes.append(pltpu.make_async_copy(buf, dst, out_sem.at[n]))

    for k in range(4):
        for o in range(0, NZ, 2):
            part = pl.ds(o, 2)
            move(xs.at[k, part], buf_x.at[k, part], out_x.at[k, part])
        for o in range(0, 1024, 512):
            part = pl.ds(o, 512)
            move(ds.at[k, part], buf_d.at[k, part], out_d.at[k, part])
    for read in reads:
        read.start()
    for read, write in zip(reads, writes):
        read.wait()
        write.start()
    for write in writes:
        write.wait()


def on_device(root_cov, row_blocks, lhat_t, diag_inv):
    anywhere = pl.BlockSpec(memory_space=pl.ANY)
    dma = pltpu.SemaphoreType.DMA
    vmem = pltpu.VMEM
    panels, diagonal = pl.pallas_call(
        kernel,
        out_shape=(
            jax.ShapeDtypeStruct((4, NZ, NX, 32, 256), F32),
            jax.ShapeDtypeStruct((4, 1024, 128), F32),
        ),
        in_specs=[pl.BlockSpec(memory_space=pltpu.SMEM), anywhere, anywhere, anywhere],
        out_specs=(anywhere, anywhere),
        scratch_shapes=[
            vmem((128, 512), F32),
            vmem((4, 32, 256), F32),
            vmem((4, 128, 128), F32),
            vmem((4, 128, 128), F32),
            vmem((4, 2, 128, 128), F32),
            vmem((8, 32, 256), F32),
            vmem((8, 3, 32, 256), F32),
            vmem((8, 32, 256), F32),
            vmem((2, 256, 128), F32),
            vmem((2, 8, 32, 128), F32),
            vmem((2, 8, 32, 128), F32),
            vmem((8, 128, 128), F32),
            vmem((1024, 128), F32),
            vmem((4, 8, 32, 256), F32),
            vmem((3, 2, 64, 1024), BF16),
            vmem((3, 2, 1024, 64), BF16),
            vmem((4, 2, 8, 4, 32, 128), F32),
            vmem((4, 8, 4, 32, 128), F32),
            vmem((4, 1024, 128), F32),
            vmem((3, 8, 128, 128), F32),
            vmem((4, 8, 32, 128), F32),
            vmem((4, 8, 32, 128), F32),
            vmem((32, 128), F32),
            vmem((128, 32), F32),
            dma((3,)),
            dma((2, 2)),
            dma((2,)),
            dma((2,)),
            dma((2,)),
            dma((2, 2)),
            dma((2,)),
            dma((4,)),
            dma((4, 2, 4)),
            dma((4, 2)),
            dma((3, 2)),
            dma((12, 8)),
            dma((12,)),
            dma((12,)),
            dma((12,)),
            dma((12,)),
            dma((4, 3)),
        ],
        compiler_params=pltpu.CompilerParams(
            collective_id=0, has_side_effects=True, vmem_limit_bytes=60 << 20
        ),
        name="selinv",
    )(row_blocks, root_cov, lhat_t, diag_inv)
    panels, diagonal = pl.pallas_call(
        hand_over,
        out_shape=(
            jax.ShapeDtypeStruct((4, NZ, NX, 32, 256), F32),
            jax.ShapeDtypeStruct((4, 1024, 128), F32),
        ),
        in_specs=[anywhere, anywhere],
        out_specs=(anywhere, anywhere),
        scratch_shapes=[
            vmem((4, NZ, NX, 32, 256), F32),
            vmem((4, 1024, 128), F32),
            dma((24,)),
            dma((24,)),
        ],
        compiler_params=pltpu.CompilerParams(vmem_limit_bytes=60 << 20),
        name="hand_over",
    )(panels, diagonal)
    return panels.reshape(4, 1024, 256), diagonal


def solution(mesh):
    return jax.shard_map(
        on_device,
        mesh=mesh,
        in_specs=(P("prow", "pcol"), P(), P(None, "prow", "pcol"), P(None, None, "pcol")),
        out_specs=(P(None, None, "pcol"), P(None, None, "pcol")),
        check_vma=False,
    )
```

```python
import jax
import jax.numpy as jnp
from jax import lax
from jax.experimental import pallas as pl
from jax.experimental.pallas import tpu as pltpu
from jax.sharding import PartitionSpec as P

MESH = pl.DeviceIdType.MESH
NZ = 8
NX = 4
NQ = 8
F32 = jnp.float32
BF16 = jnp.bfloat16
KEEP = (32, 32, 32)
EARLY = 4


def dev(p, q):
    return {"prow": p, "pcol": q}


def copy_to(src, dst, send, recv, device):
    return pltpu.make_async_remote_copy(
        src_ref=src, dst_ref=dst, send_sem=send, recv_sem=recv, device_id=device, device_id_type=MESH
    )


def halves(x):
    hi = x.astype(BF16)
    lo = (x - hi.astype(F32)).astype(BF16)
    return hi, lo


def stacked(x):
    return jnp.concatenate(halves(x), axis=0)


def dot_nn(a, b):
    return jnp.dot(a, b, preferred_element_type=F32)


def dot_nt(a, b):
    return lax.dot_general(a, b, (((1,), (1,)), ((), ())), preferred_element_type=F32)


def rows(i, n):
    return pl.ds(pl.multiple_of(i * n, n), n)


def kernel(
    rb, root_h, lhat_h, dinv_h, out_x, out_d,
    root, lhat, dblk, dturn, cls, lrow0, lrow, lx, az, xp, xr, bsel, xsel,
    lc, lsp, ltt, xo, ed, do, turn, gs, gr, held, tall,
    in_sem, cls_sem, row0_sem, row_sem, lx_sem, xr_sem, b_sem, lc_send, lc_recv, g_sem, t_sem,
    z_recv, x_recv, c_recv, b_recv, ag_send, o_sem,
):
    p = lax.axis_index("prow")
    q = lax.axis_index("pcol")
    z, x = p // NX, p % NX
    me = dev(p, q)
    par, quarter = z % 2, z // 2

    loads = [
        pltpu.make_async_copy(root_h, root, in_sem.at[0]),
        pltpu.make_async_copy(lhat_h, lhat, in_sem.at[1]),
        pltpu.make_async_copy(dinv_h.at[:, rows(z, 128), :], dblk, in_sem.at[2]),
    ]
    for load in loads:
        load.start()

    def to_z(d):
        return dev((z + d) % NZ * NX + x, q)

    def to_x(e):
        return dev(z * NX + (x + e) % NX, q)

    def to_q(e):
        return dev(p, (q + e) % NQ)

    def loop(a, b, body):
        def run(i, c):
            body(i)
            return c

        lax.fori_loop(a, b, run, 0)

    barrier = pltpu.get_barrier_semaphore()
    loop(1, NZ, lambda d: pl.semaphore_signal(barrier, inc=1, device_id=to_z(d), device_id_type=MESH))
    loop(1, NX, lambda e: pl.semaphore_signal(barrier, inc=1, device_id=to_x(e), device_id_type=MESH))
    loop(1, NQ, lambda e: pl.semaphore_signal(barrier, inc=1, device_id=to_q(e), device_id_type=MESH))

    loop(
        1, NX,
        lambda e: pl.semaphore_signal(
            barrier, inc=1, device_id=dev((2 * quarter + 1 - par) * NX + (x + e) % NX, q), device_id_type=MESH
        ),
    )

    def got(ref, recv):
        copy_to(ref, ref, recv, recv, me).wait_recv()

    def sent(ref, send):
        copy_to(ref, ref, send, send, me).wait_send()

    loads[0].wait()
    g = par * NX + x
    for c in range(2):
        mine = rb[0, 2 * q + c]
        col = root[:, 0:128]
        for m in range(1, 4):
            col = jnp.where(mine == 32 + 8 * m + q, root[:, 128 * m : 128 * m + 128], col)
        cls[quarter, c] = col
    loads[1].wait()
    pl.semaphore_wait(barrier, NZ + NX + NQ)

    def send_class(c):
        ref = cls.at[quarter, c]
        for e in (2, 1, 3):
            copy_to(ref, ref, cls_sem.at[c, 0], cls_sem.at[c, 1], to_z(2 * e)).start()

    send_class(1)
    loop(1, NQ, lambda e: copy_to(lhat.at[0], lrow0.at[q], row0_sem.at[0], row0_sem.at[1], to_q(e)).start())
    loop(
        1, NQ,
        lambda e: copy_to(lhat.at[pl.ds(1, 3)], lrow.at[q], row_sem.at[0], row_sem.at[1], to_q(e)).start(),
    )
    lrow0[q] = lhat[0]
    lrow[q] = lhat[1:4]
    for k in range(4):
        lc[k, z] = lhat[k]

    def lc_hop(k, far):
        for side, d in ((0, 1), (1, NZ - 1)):
            if far == 3 and side == 1:
                continue
            ref = lc.at[k, (z + NZ - far * d) % NZ]
            if far > 0:
                got(ref, lc_recv.at[k, side, far - 1])
            copy_to(ref, ref, lc_send.at[k], lc_recv.at[k, side, far], to_z(d)).start()

    def got_lc(k):
        got(lc.at[k, 0], lc_recv.at[k, 1, 2])
        got(lc.at[k, 0], lc_recv.at[k, 0, 3])

    def order(i):
        h = i // 2 + 1
        return h + (i % 2) * (NZ - 2 * h)

    got(lrow0.at[pl.ds(0, 7)], row0_sem.at[1])

    def to_group(e, body):
        o = (g + e) % NQ
        body(o, dev((2 * quarter + o // NX) * NX + o % NX, q))

    def lx_peer(e):
        to_group(
            e, lambda o, d: copy_to(lrow0.at[o], lx.at[g], lx_sem.at[0], lx_sem.at[1], d).start()
        )

    loop(1, NQ, lx_peer)
    send_class(0)
    lx[g] = lrow0[g]
    lc_hop(0, 0)

    def turn_dinv(k):
        dturn[k] = dblk[k].T


    def prepare(k):
        for o in range(NQ):
            for h in range(2):
                hi, lo = halves(lrow[o, k, :, 128 * h : 128 * h + 128])
                lsp[k, h, 0:32, 128 * o : 128 * o + 128] = hi
                lsp[k, h, 32:64, 128 * o : 128 * o + 128] = lo

    def prepare_t(k):
        for o in range(NQ):
            for h in range(2):
                v = lrow[o, k, :, 128 * h : 128 * h + 128]
                ltt[k, h, 128 * o : 128 * o + 128, :] = jnp.concatenate(halves(v.T), axis=1)

    def buf_of(k, c):
        return (xo.at[k, c], 3 * k + c, KEEP[c]) if c < 2 else (ed.at[k], 3 * k + 2, KEEP[2])

    def start_gather(k, c):
        buf, n, keep = buf_of(k, c)
        ref = buf.at[z, x]
        for e in (2, 1, 3):
            copy_to(ref, ref, ag_send.at[n], c_recv.at[n], to_x(e)).start()
        top = buf.at[z, x, pl.ds(0, keep), :]

        def one(i):
            d = order(6 - i)
            copy_to(top, top, ag_send.at[n], z_recv.at[n, d], to_z(d)).start()

        loop(0, NZ - 1, one)

    def got_near(k, c):
        buf, n, keep = buf_of(k, c)
        got(buf.at[0, pl.ds(0, 3)], c_recv.at[n])

    def second_part(k, c):
        buf, n, keep = buf_of(k, c)
        if keep < 32:
            ref = buf.at[z, :, pl.ds(keep, 32 - keep), :]
            loop(
                0, NZ - 1,
                lambda i: copy_to(ref, ref, ag_send.at[n], b_recv.at[n], to_z(order(6 - i))).start(),
            )

    def forward(k, c, first, last):
        buf, n, keep = buf_of(k, c)

        def one(i):
            d = order(i)
            ref = buf.at[(z + NZ - d) % NZ, x, pl.ds(0, keep), :]
            got(ref, z_recv.at[n, d])
            loop(1, NX, lambda e: copy_to(ref, ref, ag_send.at[n], x_recv.at[n], to_x(e)).start())

        loop(first, last, one)

    def got_all(k, c):
        buf, n, keep = buf_of(k, c)
        got(buf.at[pl.ds(0, 7), pl.ds(0, 3), pl.ds(0, keep), :], x_recv.at[n])
        if keep < 32:
            got(buf.at[pl.ds(0, 7), :, pl.ds(keep, 32 - keep), :], b_recv.at[n])

    def put_x(k, c, value):
        xo[k, c, z, x] = value
        start_gather(k, c)

    got(lx.at[pl.ds(0, 7)], lx_sem.at[1])
    left, left_low = halves(lx[...].reshape(256, 256))
    for c in (1, 0):
        got(cls.at[pl.ds(0, 3), c], cls_sem.at[c, 1])
        if c == 0:
            lc_hop(0, 1)
        for t in range(2):
            want = rb[0, 2 * g + t]
            blk = cls[0, c]
            for o in range(1, 4):
                blk = jnp.where(want == 32 + 8 * o + g, cls[o, c], blk)
            az[c, 128 * t : 128 * t + 128, :] = blk
        hi, lo = halves(az[c])
        total = dot_nn(left, hi) + dot_nn(left_low, hi) + dot_nn(left, lo)
        xp[c] = total.reshape(NQ, 32, 128)
        for e in range(1, NQ):
            to_group(
                e, lambda o, d: copy_to(xp.at[c, o], xr.at[c, g], xr_sem.at[c, 0], xr_sem.at[c, 1], d).start()
            )
        xr[c, g] = xp[c, g]

    second = rb[1, 2 * q + 1] == rb[0, 2 * q + 1]
    low = rb[1, 2 * g + 1] == rb[0, 2 * g + 1]
    top = jnp.where(second, az[1, 0:128], az[0, 0:128])
    bot = jnp.where(second, az[1, 128:256], az[0, 128:256])
    bsel[g] = jnp.where(low, bot, top)
    b_own = bsel.at[g]

    def b_peer(e):
        to_group(e, lambda o, d: copy_to(b_own, b_own, b_sem.at[0], b_sem.at[1], d).start())

    def put_first(c):
        got(xr.at[c, pl.ds(0, 7)], xr_sem.at[c, 1])
        first = -xr[c, 0]
        for o in range(1, NQ):
            first = first - xr[c, o]
        put_x(0, c, first)

    put_first(1)
    loads[2].wait()
    loop(0, 4, turn_dinv)
    got(lrow.at[pl.ds(0, 7)], row_sem.at[1])
    prepare(0)
    prepare_t(0)
    lc_hop(0, 2)
    lc_hop(0, 3)
    put_first(0)
    loop(1, NQ, b_peer)

    def times_split(left_rows, value):
        hi, lo = halves(value)
        both = dot_nn(left_rows[...], hi)
        return both[0:32] + both[32:64] + dot_nn(left_rows[0:32], lo)

    def times_turned(right, lefts):
        acc = jnp.zeros((256, 64), F32)
        for i, v in enumerate(lefts):
            acc = acc + dot_nn(stacked(v), right[256 * i : 256 * i + 256, :])
        return acc[0:128, 0:32] + acc[0:128, 32:64] + acc[128:256, 0:32]

    forward(0, 1, 0, 7)

    def step(k, carry):
        if KEEP[1] == 32:
            got_near(k, 1)
        else:

            @pl.when(k == 0)
            def _():
                got_near(k, 1)

        got_near(k, 0)
        got_lc(k)
        xh, xl = halves(
            jnp.concatenate([xo[k, 0, z].reshape(128, 128), xo[k, 1, z].reshape(128, 128)], axis=1)
        )
        ch, cl = halves(lc[k].reshape(256, 256))
        part = dot_nt(ch, xh) + dot_nt(cl, xh) + dot_nt(ch, xl)
        gs[k] = part.reshape(NQ, 32, 128)

        def g_peer(e):
            copy_to(gs.at[k, (q + e) % NQ], gr.at[k, q], g_sem.at[k, 0], g_sem.at[k, 1], to_q(e)).start()

        for e in (4, 3, 5, 2, 6, 1, 7):
            g_peer(e)
        gr[k, q] = gs[k, q]
        second_part(k, 0)

        @pl.when(k == 0)
        def _():
            second_part(k, 1)

        forward(k, 0, 0, 7)

        @pl.when(k < 3)
        def _():
            lc_hop(k + 1, 0)

        @pl.when(k == 0)
        def _():
            got(bsel.at[pl.ds(0, 7)], b_sem.at[1])
            sent(bsel.at[pl.ds(0, 7)], b_sem.at[0])
            held[...] = times_split(lsp.at[0, 1], bsel[...].reshape(1024, 128))

        got(gr.at[k, pl.ds(0, 7)], g_sem.at[k, 1])
        total = gr[k, 0]
        for o in range(1, NQ):
            total = total + gr[k, o]
        ed[k, z, x] = dturn[k, rows(x, 32), :] - total
        start_gather(k, 2)
        forward(k, 2, 0, EARLY)
        if KEEP[2] < 32:
            got_near(k, 2)
            second_part(k, 2)

        @pl.when(k < 3)
        def _():
            lc_hop(k + 1, 1)

        got_all(k, 1)
        got_all(k, 0)

        @pl.when(k < 3)
        def _():
            pick = rb[k + 1, 2 * q + 1] == rb[k, 2 * q + 1]
            xsel[...] = jnp.where(pick, xo[k, 1].reshape(1024, 128), xo[k, 0].reshape(1024, 128))

            def t_peer(e):
                copy_to(
                    xsel.at[rows((q + e) % NQ, 128), :], turn.at[k, q], t_sem.at[k, 0], t_sem.at[k, 1], to_q(e)
                ).start()

            loop(1, NQ, t_peer)
            turn[k, q] = xsel[rows(q, 128), :]
            put_x(k + 1, 1, -(held[...] + times_split(lsp.at[k, 0], xsel[...])))

        forward(k, 2, EARLY, 7)
        for c in range(2):
            pltpu.make_async_copy(
                xo.at[k, c], out_x.at[k, :, :, :, pl.ds(128 * c, 128)], o_sem.at[k, c]
            ).start()

        @pl.when(k < 2)
        def _():
            prepare(k + 1)
            prepare_t(k + 1)

        @pl.when(k < 3)
        def _():
            lc_hop(k + 1, 2)
            got(turn.at[k, pl.ds(0, 7)], t_sem.at[k, 1])
            sent(turn.at[k, pl.ds(0, 7)], t_sem.at[k, 0])
            tall[...] = times_turned(
                ltt.at[k, 1], [jnp.concatenate([turn[k, o], turn[k, o + 1]], axis=1) for o in range(0, NQ, 2)]
            )
            lc_hop(k + 1, 3)
            if KEEP[1] < 32:
                got_near(k + 1, 1)
                second_part(k + 1, 1)

        if KEEP[2] == 32:
            got_near(k, 2)
        got_all(k, 2)

        @pl.when(k < 3)
        def _():
            new = tall[...] + times_turned(
                ltt.at[k, 0],
                [
                    jnp.concatenate([ed[k, o].reshape(128, 128), ed[k, o + 1].reshape(128, 128)], axis=1)
                    for o in range(0, NQ, 2)
                ],
            )
            put_x(k + 1, 0, -new.T)
            forward(k + 1, 1, 0, 7)

        for o in range(NQ):
            do[k, 128 * o : 128 * o + 128, :] = ed[k, o].reshape(128, 128).T
        pltpu.make_async_copy(do.at[k], out_d.at[k], o_sem.at[k, 2]).start()

        @pl.when(k < 2)
        def _():
            pick = rb[k + 2, 2 * q + 1] == rb[k + 1, 2 * q + 1]
            for o in range(NQ):
                lower = rb[k + 2, 2 * o + 1] == rb[k + 1, 2 * o + 1]
                span = slice(128 * o, 128 * o + 128)
                upper_part = jnp.where(pick, xsel[span, :], do[k, span, :])
                lower_part = jnp.where(pick, bsel[o], turn[k, o].T)
                bsel[o] = jnp.where(lower, lower_part, upper_part)
            held[...] = times_split(lsp.at[k + 1, 1], bsel[...].reshape(1024, 128))

        return carry

    lax.fori_loop(0, 4, step, 0)

    def finish(k):
        for c in range(3):
            sent(do.at[k, pl.ds(0, 992), :], ag_send.at[3 * k + c])
        for c in range(2):
            pltpu.make_async_copy(
                xo.at[k, c], out_x.at[k, :, :, :, pl.ds(128 * c, 128)], o_sem.at[k, c]
            ).wait()
        sent(gr.at[k, pl.ds(0, 7)], g_sem.at[k, 0])
        sent(lc.at[k, pl.ds(0, 7)], lc_send.at[k])
        pltpu.make_async_copy(do.at[k], out_d.at[k], o_sem.at[k, 2]).wait()

    loop(0, 4, finish)
    for c in range(2):
        sent(cls.at[pl.ds(0, 3), c], cls_sem.at[c, 0])
        sent(xr.at[c, pl.ds(0, 7)], xr_sem.at[c, 0])
    sent(lrow0.at[pl.ds(0, 7)], row0_sem.at[0])
    sent(lrow.at[pl.ds(0, 7)], row_sem.at[0])
    sent(lx.at[pl.ds(0, 7)], lx_sem.at[0])


def hand_over(xs, ds, out_x, out_d, buf_x, buf_d, in_sem, out_sem):
    reads, writes = [], []

    def move(src, buf, dst):
        n = len(reads)
        reads.append(pltpu.make_async_copy(src, buf, in_sem.at[n]))
        writes.append(pltpu.make_async_copy(buf, dst, out_sem.at[n]))

    for k in range(4):
        for o in range(0, NZ, 2):
            part = pl.ds(o, 2)
            move(xs.at[k, part], buf_x.at[k, part], out_x.at[k, part])
        for o in range(0, 1024, 512):
            part = pl.ds(o, 512)
            move(ds.at[k, part], buf_d.at[k, part], out_d.at[k, part])
    for read in reads:
        read.start()
    for read, write in zip(reads, writes):
        read.wait()
        write.start()
    for write in writes:
        write.wait()


def on_device(root_cov, row_blocks, lhat_t, diag_inv):
    anywhere = pl.BlockSpec(memory_space=pl.ANY)
    dma = pltpu.SemaphoreType.DMA
    vmem = pltpu.VMEM
    panels, diagonal = pl.pallas_call(
        kernel,
        out_shape=(
            jax.ShapeDtypeStruct((4, NZ, NX, 32, 256), F32),
            jax.ShapeDtypeStruct((4, 1024, 128), F32),
        ),
        in_specs=[pl.BlockSpec(memory_space=pltpu.SMEM), anywhere, anywhere, anywhere],
        out_specs=(anywhere, anywhere),
        scratch_shapes=[
            vmem((128, 512), F32),
            vmem((4, 32, 256), F32),
            vmem((4, 128, 128), F32),
            vmem((4, 128, 128), F32),
            vmem((4, 2, 128, 128), F32),
            vmem((8, 32, 256), F32),
            vmem((8, 3, 32, 256), F32),
            vmem((8, 32, 256), F32),
            vmem((2, 256, 128), F32),
            vmem((2, 8, 32, 128), F32),
            vmem((2, 8, 32, 128), F32),
            vmem((8, 128, 128), F32),
            vmem((1024, 128), F32),
            vmem((4, 8, 32, 256), F32),
            vmem((3, 2, 64, 1024), BF16),
            vmem((3, 2, 1024, 64), BF16),
            vmem((4, 2, 8, 4, 32, 128), F32),
            vmem((4, 8, 4, 32, 128), F32),
            vmem((4, 1024, 128), F32),
            vmem((3, 8, 128, 128), F32),
            vmem((4, 8, 32, 128), F32),
            vmem((4, 8, 32, 128), F32),
            vmem((32, 128), F32),
            vmem((128, 32), F32),
            dma((3,)),
            dma((2, 2)),
            dma((2,)),
            dma((2,)),
            dma((2,)),
            dma((2, 2)),
            dma((2,)),
            dma((4,)),
            dma((4, 2, 4)),
            dma((4, 2)),
            dma((3, 2)),
            dma((12, 8)),
            dma((12,)),
            dma((12,)),
            dma((12,)),
            dma((12,)),
            dma((4, 3)),
        ],
        compiler_params=pltpu.CompilerParams(
            collective_id=0, has_side_effects=True, vmem_limit_bytes=60 << 20
        ),
        name="selinv",
    )(row_blocks, root_cov, lhat_t, diag_inv)
    panels, diagonal = pl.pallas_call(
        hand_over,
        out_shape=(
            jax.ShapeDtypeStruct((4, NZ, NX, 32, 256), F32),
            jax.ShapeDtypeStruct((4, 1024, 128), F32),
        ),
        in_specs=[anywhere, anywhere],
        out_specs=(anywhere, anywhere),
        scratch_shapes=[
            vmem((4, NZ, NX, 32, 256), F32),
            vmem((4, 1024, 128), F32),
            dma((24,)),
            dma((24,)),
        ],
        compiler_params=pltpu.CompilerParams(vmem_limit_bytes=60 << 20),
        name="hand_over",
    )(panels, diagonal)
    return panels.reshape(4, 1024, 256), diagonal


def solution(mesh):
    return jax.shard_map(
        on_device,
        mesh=mesh,
        in_specs=(P("prow", "pcol"), P(), P(None, "prow", "pcol"), P(None, None, "pcol")),
        out_specs=(P(None, None, "pcol"), P(None, None, "pcol")),
        check_vma=False,
    )
```
